128 devices in a mesh: nodes: 32 (over y, x, core), hid: 4 (over z).
Axes of the slice: x: 4, y: 4, z: 4, core: 2. Of those that a mesh axis runs over, the one named last changes fastest.
Arguments:
- node_features: bfloat16 [32768, 512], P('nodes', 'hid'), may hold values from -6 to 6
- w_out: bfloat16 [512, 512], P(None, 'hid'), may hold values from -0.25 to 0.25
- w_in: bfloat16 [512, 512], P(None, 'hid'), may hold values from -0.25 to 0.25
- w_self: bfloat16 [512, 512], P(None, 'hid'), may hold values from -0.25 to 0.25
- cotangent: bfloat16 [32768, 512], P('nodes', 'hid'), may hold values from -6 to 6
- tile_src: int32 [8192], P('nodes'), may hold values from 0 to 255, as said below
- tile_dst: int32 [8192], P('nodes'), may hold values from 0 to 255, as said below
- tile_pattern: int32 [8192, 128, 128], P('nodes'), may hold values 0 or 1
- tile_count: int32 [32], P('nodes'), may hold values from 64 to 256, as said below
Outputs:
- hidden: bfloat16 [32768, 512], P('nodes', 'hid')
- grad_input: bfloat16 [32768, 512], P('nodes', 'hid')
- grad_w_out: float32 [512, 512], P('nodes', 'hid')
- grad_w_in: float32 [512, 512], P('nodes', 'hid')
- grad_w_self: float32 [512, 512], P('nodes', 'hid')
The draws below stay inside these ranges and needn't reach their ends.
Inputs may be any that keep to these rules, and one draw needn't show every extreme that they name: `tile_src`: every slot of device d names a source row block of device d itself, that is d * 8 to d * 8 + 7. `tile_dst`: among the used slots of device d, at most 2 have a destination block held by any one other device, and exactly 2 for each of the devices just before and just after d along nodes, taken cyclically. `tile_count`: some device uses all 256 slots.
All inputs are finite; a program needn't handle non-finite values. No bound on the sum of `tile_pattern` on one device may be relied on, other than what follows from the above.
Results may differ from the reference program's by a relative error of at most 0.0055.
Values may be sent and summed in bfloat16 or wider, within the bound.
No kernel may reach another device: no remote copies, remote signals or barrier semaphores. Data moves between devices by JAX's collectives and lax.ppermute only.
A program may use at most 128 MiB of HBM per device.

```python
import jax
import jax.numpy as jnp
from jax import lax

D = 512
BLK = 128
NB_DEV = 8
TILES_DEV = 256
CAP = 2
NODES = 32768
TILES = 8192
N_NODES = 32


def layout(key):
    keys = jax.random.split(key, 7)
    spread_counts = jax.random.randint(keys[0], (N_NODES, N_NODES), 0, CAP + 1)
    spread_counts = spread_counts.at[:, 0].set(0)
    spread_counts = spread_counts.at[:, 1].set(CAP)
    spread_counts = spread_counts.at[:, N_NODES - 1].set(CAP)
    remote_total = jnp.sum(spread_counts, axis=1)
    running = jnp.cumsum(spread_counts, axis=1)
    slot_ids = jnp.arange(TILES_DEV, dtype=jnp.int32)
    base_offset = jnp.sum((slot_ids[None, :, None] >= running[:, None, :]).astype(jnp.int32), axis=2)
    base_offset = jnp.where(slot_ids[None, :] < remote_total[:, None], base_offset, 0)
    divisor = 1 + jax.random.randint(keys[1], (N_NODES,), 0, 4)
    used = jnp.maximum(TILES_DEV // divisor, remote_total)
    busiest = jax.random.randint(keys[2], (), 0, N_NODES)
    used = jnp.where(jnp.arange(N_NODES) == busiest, TILES_DEV, used)
    shuffles = jax.vmap(lambda single: jax.random.permutation(single, TILES_DEV))(jax.random.split(keys[3], N_NODES))
    sort_keys = jnp.where(slot_ids[None, :] < used[:, None], shuffles, TILES_DEV + slot_ids[None, :])
    order = jnp.argsort(sort_keys, axis=1)
    offset = jnp.take_along_axis(base_offset, order, axis=1)
    garbage = jax.random.randint(keys[4], (N_NODES, TILES_DEV), 0, N_NODES)
    offset = jnp.where(slot_ids[None, :] < used[:, None], offset, garbage)
    devices = jnp.arange(N_NODES, dtype=jnp.int32)[:, None]
    owner_dev = (devices + offset) % N_NODES
    targets = owner_dev * NB_DEV + jax.random.randint(keys[5], (N_NODES, TILES_DEV), 0, NB_DEV)
    sources = devices * NB_DEV + jax.random.randint(keys[6], (N_NODES, TILES_DEV), 0, NB_DEV)
    return (sources.reshape(-1).astype(jnp.int32), targets.reshape(-1).astype(jnp.int32), used.astype(jnp.int32))


def draw_tile_src(key, part):
    sources, targets, used = layout(key)
    return sources


def draw_tile_dst(key, part):
    sources, targets, used = layout(key)
    return targets


def draw_tile_count(key, part):
    sources, targets, used = layout(key)
    return used


def set_ends(result, stream_key, least, largest):
    longest = result.shape.index(max(result.shape))
    spots = []
    for shift in (0, 1):
        where = [jax.random.randint(jax.random.fold_in(stream_key, axis), (), 0, length) for axis, length in enumerate(result.shape)]
        where[longest] = (where[longest] + shift) % result.shape[longest]
        spots.append(tuple(where))
    return result.at[spots[0]].set(least).at[spots[1]].set(largest)


def with_spikes(drawn, own_key, source, target, shards_of, factor):
    def block_of(dim):
        return (jnp.arange(drawn.shape[dim]) // (drawn.shape[dim] // shards_of)).reshape((-1,) + (1,) * (drawn.ndim - 1 - dim))

    first = jax.random.permutation(own_key, shards_of)[block_of(target)]
    far = (block_of(target) + shards_of // 2) % shards_of
    return jnp.where((block_of(source) == first) | (block_of(source) == far), factor * drawn, drawn)


def block_scale(stream_key, extent, shards, least, largest):
    factor_of, own = 1.0, jax.random.fold_in(stream_key, 6)
    for dim, blocks in shards:
        heights = jnp.exp(jax.random.uniform(jax.random.fold_in(own, dim), (blocks,), jnp.float32, least / len(shards), largest / len(shards)))
        factor_of = factor_of * jnp.repeat(heights, extent[dim] // blocks).reshape([-1 if axis == dim else 1 for axis in range(len(extent))])
    return factor_of


def noise(rng, shape, scale, reach, pieces=(), kind=jnp.bfloat16):
    values = jax.random.normal(rng, shape, jnp.float32) * scale
    if len(pieces) > 0:
        values = block_scale(rng, shape, pieces, -0.22, 0.18) * values
    return jnp.clip(values, min=-reach, max=reach).astype(kind)


def noise_with(stream_key, dims, deviation, most, shards, heavy, held_as=jnp.bfloat16):
    entries = deviation * jax.random.normal(stream_key, dims, jnp.float32)
    if shards:
        entries = entries * block_scale(stream_key, dims, shards, -0.22, 0.18)
    return jnp.clip(with_spikes(entries, jax.random.fold_in(stream_key, 3), *heavy), -most, most).astype(held_as)


def setup_inputs(seed: int = 0) -> dict:
    arg_keys = jax.random.split(jax.random.key(seed), 10)
    return {
        "node_features": noise_with(arg_keys[0], (NODES, D), 1.0, 6.0, ((0, 32), (1, 4)), (0, 1, 32, 2.75)),
        "w_out": noise(arg_keys[1], (D, D), D ** -0.5, 0.25, ((1, 4),)),
        "w_in": noise(arg_keys[2], (D, D), D ** -0.5, 0.25, ((1, 4),)),
        "w_self": noise(arg_keys[3], (D, D), D ** -0.5, 0.25, ((1, 4),)),
        "cotangent": noise(arg_keys[4], (NODES, D), 1.0, 6.0, ((0, 32), (1, 4))),
        "tile_src": draw_tile_src(jax.random.fold_in(arg_keys[9], 71), 0),
        "tile_dst": draw_tile_dst(jax.random.fold_in(arg_keys[9], 71), 0),
        "tile_pattern": set_ends((jax.random.randint(arg_keys[7], (TILES, BLK, BLK), 0, 8) < 1).astype(jnp.int32), jax.random.fold_in(arg_keys[7], 1), 0, 1),
        "tile_count": draw_tile_count(jax.random.fold_in(arg_keys[9], 71), 0),
    }


def spread(push_feat, pull_feat, tile_src, tile_dst, tile_pattern, is_valid):
    block_total = N_NODES * NB_DEV
    push_blocks = push_feat.astype(jnp.float32).reshape(block_total, BLK, D)
    pull_blocks = pull_feat.astype(jnp.float32).reshape(block_total, BLK, D)
    tile_group = 32
    stacked = (tile_src.reshape(-1, tile_group), tile_dst.reshape(-1, tile_group),
               tile_pattern.reshape(-1, tile_group, BLK, BLK), is_valid.reshape(-1, tile_group))

    def advance(running, tile_slice):
        out_acc, in_acc = running
        sources, targets, pattern, usable = tile_slice
        weights = jnp.where(usable[:, None, None], pattern, 0).astype(jnp.float32)
        out_part = jnp.einsum("tij,tjk->tik", weights, pull_blocks[targets], precision=lax.Precision.HIGHEST)
        in_part = jnp.einsum("tji,tjk->tik", weights, push_blocks[sources], precision=lax.Precision.HIGHEST)
        return (out_acc.at[sources].add(out_part), in_acc.at[targets].add(in_part)), None

    empty = jnp.zeros((block_total, BLK, D), jnp.float32)
    (out_acc, in_acc), unused = lax.scan(advance, (empty, empty), stacked)
    return out_acc.reshape(-1, D), in_acc.reshape(-1, D)


def reference(node_features, w_out, w_in, w_self, cotangent, tile_src, tile_dst, tile_pattern, tile_count):
    slot_ids = jnp.arange(N_NODES * TILES_DEV, dtype=jnp.int32)
    is_valid = (slot_ids % TILES_DEV) < tile_count[slot_ids // TILES_DEV]
    agg_out, agg_in = spread(node_features, node_features, tile_src, tile_dst, tile_pattern, is_valid)
    prop_out = agg_out.astype(jnp.bfloat16)
    prop_in = agg_in.astype(jnp.bfloat16)
    pre_act = (jnp.dot(prop_out, w_out, preferred_element_type=jnp.float32)
               + jnp.dot(prop_in, w_in, preferred_element_type=jnp.float32)) / 32.0
    pre_act = pre_act + jnp.dot(node_features, w_self, preferred_element_type=jnp.float32)
    hidden = jax.nn.silu(pre_act).astype(jnp.bfloat16)
    sigmoid_z = jax.nn.sigmoid(pre_act)
    grad_z = (cotangent.astype(jnp.float32) * sigmoid_z * (1.0 + pre_act * (1.0 - sigmoid_z))).astype(jnp.bfloat16)
    grad_w_out = jnp.dot(prop_out.T, grad_z, preferred_element_type=jnp.float32) / 32.0
    grad_w_in = jnp.dot(prop_in.T, grad_z, preferred_element_type=jnp.float32) / 32.0
    grad_w_self = jnp.dot(node_features.T, grad_z, preferred_element_type=jnp.float32)
    back_out = (jnp.dot(grad_z, w_out.T, preferred_element_type=jnp.float32) / 32.0).astype(jnp.bfloat16)
    back_in = (jnp.dot(grad_z, w_in.T, preferred_element_type=jnp.float32) / 32.0).astype(jnp.bfloat16)
    grad_self = jnp.dot(grad_z, w_self.T, preferred_element_type=jnp.float32)
    from_in, from_out = spread(back_out, back_in, tile_src, tile_dst, tile_pattern, is_valid)
    grad_input = (grad_self + from_in + from_out).astype(jnp.bfloat16)
    return hidden, grad_input, grad_w_out, grad_w_in, grad_w_self
```

```python
import jax
import jax.numpy as jnp
from jax import lax
from jax.experimental import pallas as pl
from jax.experimental.pallas import tpu as pltpu
from jax.sharding import PartitionSpec as P

CAP = 2
GROUP = 16
BATCH = 8
CODES = 16
PICKS = 4
MIB = 1024 * 1024
ROOM = 60 * MIB
F32 = jnp.float32
BF16 = jnp.bfloat16


def split(value, size):
    shift = size.bit_length() - 1
    return jnp.right_shift(value, shift), jnp.bitwise_and(value, size - 1)


def pick_kernel(blocks, src_ref, dst_ref, info_ref, pattern_ref, away_ref, send_ref, meta_ref, tiles, counts, listed, sems):
    side = tiles.shape[1]
    devices = counts.shape[0]
    part = (send_ref.shape[1] - CODES) // CAP
    total, myself, quarter = info_ref[0], info_ref[1], info_ref[2]

    def clear(owner, carry):
        counts[owner] = 0
        for rank in range(CAP):
            meta_ref[owner * CAP + rank] = 0
        return carry

    lax.fori_loop(0, devices, clear, 0, unroll=4)

    def copy(slot, entry):
        return pltpu.make_async_copy(pattern_ref.at[slot], tiles.at[entry], sems.at[entry])

    def scan(slot, found):
        owner, _ = split(dst_ref[slot], blocks)
        listed[found] = slot
        return found + ((owner != myself) & (slot < total)).astype(jnp.int32)

    found = lax.fori_loop(0, dst_ref.shape[0], scan, 0, unroll=8)
    found = jnp.minimum(found, devices * CAP)

    def keep(entry, carry):
        slot = listed[entry]
        copy(slot, entry).start()
        owner, landing = split(dst_ref[slot], blocks)
        source = jnp.clip(src_ref[slot] - myself * blocks, 0, blocks - 1)
        rank = jnp.minimum(counts[owner], CAP - 1)
        counts[owner] = rank + 1
        place = owner * CAP + rank
        meta_ref[place] = 1 + source + blocks * landing
        listed[entry] = place
        return carry

    lax.fori_loop(0, found, keep, 0)
    row = lax.broadcasted_iota(jnp.int32, (part, side), 0)
    column = lax.broadcasted_iota(jnp.int32, (part, side), 1)
    chosen = (column == row + quarter * part).astype(F32).astype(BF16)

    def turn(batch, carry):
        first = batch * PICKS
        for index in range(PICKS):

            @pl.when(first + index < found)
            def arrive():
                copy(0, first + index).wait()

        entries = [jnp.minimum(first + index, found - 1) for index in range(PICKS)]
        values = [tiles[entry].astype(F32).astype(BF16) for entry in entries]
        turned = [
            lax.dot_general(chosen, value, (((1,), (1,)), ((), ())), preferred_element_type=F32).astype(BF16) for value in values
        ]
        for index, entry in enumerate(entries):
            place = listed[entry]
            owner, rank = split(place, CAP)
            away_ref[place] = values[index]
            send_ref[owner, pl.ds(pl.multiple_of(rank * part, part), part), :] = turned[index]
        return carry

    lax.fori_loop(0, lax.div(found + PICKS - 1, PICKS), turn, 0)
    lane = lax.broadcasted_iota(jnp.int32, (CODES, side), 1)

    def code(owner, carry):
        values = jnp.zeros((CODES, side), jnp.int32)
        for rank in range(CAP):
            values = jnp.where(lane == rank, meta_ref[owner * CAP + rank], values)
        send_ref[owner, CAP * part :, :] = values.astype(F32).astype(BF16)
        return carry

    lax.fori_loop(0, devices, code, 0, unroll=4)


def pick(tile_src, tile_dst, info, tile_pattern, blocks, devices, quarters):
    side = tile_pattern.shape[1]
    places = devices * CAP
    vmem = pl.BlockSpec(memory_space=pltpu.VMEM)
    smem = pl.BlockSpec(memory_space=pltpu.SMEM)
    return pl.pallas_call(
        lambda *refs: pick_kernel(blocks, *refs),
        in_specs=[smem, smem, smem, pl.BlockSpec(memory_space=pltpu.HBM)],
        out_specs=[vmem, vmem, smem],
        out_shape=[
            jax.ShapeDtypeStruct((places, side, side), BF16),
            jax.ShapeDtypeStruct((devices, CAP * side // quarters + CODES, side), BF16),
            jax.ShapeDtypeStruct((places,), jnp.int32),
        ],
        scratch_shapes=[
            pltpu.VMEM((places, side, side), jnp.int32),
            pltpu.SMEM((devices,), jnp.int32),
            pltpu.SMEM((tile_src.shape[0] + 1,), jnp.int32),
            pltpu.SemaphoreType.DMA((places,)),
        ],
        compiler_params=pltpu.CompilerParams(vmem_limit_bytes=ROOM),
        cost_estimate=pl.CostEstimate(flops=places * side * side, bytes_accessed=8 * MIB, transcendentals=0),
        name="pick",
    )(tile_src, tile_dst, info, tile_pattern)


def pile_kernel(src_ref, dst_ref, info_ref, pattern_ref, local_ref, acc, groups, sems):
    depth, group, side = groups.shape[0], groups.shape[1], groups.shape[2]
    blocks = local_ref.shape[0] // side
    total, myself = info_ref[0], info_ref[1]
    turns = lax.div(total + group - 1, group)

    def copy(turn):
        return pltpu.make_async_copy(pattern_ref.at[pl.ds(turn * group, group)], groups.at[turn], sems.at[turn])

    for turn in range(depth):

        @pl.when(turn < turns)
        def begin():
            copy(turn).start()

    def clear(pair, carry):
        acc[pair] = jnp.zeros((side, side), jnp.int32)
        return carry

    lax.fori_loop(0, acc.shape[0], clear, 0)

    def take(turn, carry):
        copy(turn).wait()

        def add(index, carry):
            slot = turn * group + index
            source = jnp.clip(src_ref[slot] - myself * blocks, 0, blocks - 1)
            owner, landing = split(dst_ref[slot], blocks)
            pair = jnp.where((owner == myself) & (slot < total), source * blocks + landing, blocks * blocks)
            acc[pair] = acc[pair] + groups[turn, index]
            return carry

        lax.fori_loop(0, group, add, 0, unroll=4)
        return carry

    lax.fori_loop(0, turns, take, 0)

    def finish(source, carry):
        rows = pl.ds(pl.multiple_of(source * side, side), side)
        for landing in range(blocks):
            local_ref[rows, landing * side : (landing + 1) * side] = acc[source * blocks + landing].astype(F32).astype(BF16)
        return carry

    lax.fori_loop(0, blocks, finish, 0)


def pile(tile_src, tile_dst, info, tile_pattern, blocks):
    slots, side = tile_pattern.shape[0], tile_pattern.shape[1]
    smem = pl.BlockSpec(memory_space=pltpu.SMEM)
    return pl.pallas_call(
        pile_kernel,
        in_specs=[smem, smem, smem, pl.BlockSpec(memory_space=pltpu.HBM)],
        out_specs=pl.BlockSpec(memory_space=pltpu.VMEM),
        out_shape=jax.ShapeDtypeStruct((blocks * side, blocks * side), BF16),
        scratch_shapes=[
            pltpu.VMEM((blocks * blocks + 1, side, side), jnp.int32),
            pltpu.VMEM((slots // GROUP, GROUP, side, side), jnp.int32),
            pltpu.SemaphoreType.DMA((slots // GROUP,)),
        ],
        compiler_params=pltpu.CompilerParams(vmem_limit_bytes=ROOM),
        cost_estimate=pl.CostEstimate(flops=slots * side * side, bytes_accessed=slots * side * side * 4, transcendentals=0),
        name="pile",
    )(tile_src, tile_dst, info, tile_pattern)


def list_products(info_ref, sent_ref, got_ref, list_ref, blocks):
    x, y, core = info_ref[3], info_ref[4], info_ref[5]
    places = sent_ref.shape[0]
    half = blocks // 2
    last = list_ref.shape[0] - 2

    def entry(device, block, place, row):
        chip, their_core = split(device, 2)
        their_y, their_x = split(chip, 4)
        step_x, step_y = jnp.bitwise_and(x - their_x, 3), jnp.bitwise_and(y - their_y, 3)
        track, block = split(block, half)
        first = jnp.where(track == 0, step_x, step_y)
        second = jnp.where(track == 0, step_y, step_x)
        index = ((second * 4 + first) * 2 + jnp.bitwise_xor(their_core, track)) * half + block
        index = index + jnp.where(track == core, 0, 32 * half)
        return (index * 64 + place) * 32 + row

    def out(place, count):
        code = sent_ref[place] - 1
        landing, source = split(jnp.maximum(code, 0), blocks)
        list_ref[count] = entry(jnp.right_shift(place, 1), landing, place, source)
        return count + (code >= 0).astype(jnp.int32)

    def into(place, count):
        code = got_ref[jnp.right_shift(place, 1), jnp.bitwise_and(place, 1)] - 1
        landing, source = split(jnp.maximum(code, 0), blocks)
        list_ref[count] = entry(jnp.right_shift(place, 1), source, place, blocks + landing)
        return count + (code >= 0).astype(jnp.int32)

    def padded(count):
        ends = lax.div(count + BATCH - 1, BATCH) * BATCH

        def pad(index, carry):
            list_ref[index] = 2 * blocks
            return carry

        lax.fori_loop(count, ends, pad, 0)
        return ends

    count = padded(lax.fori_loop(0, places, out, 0, unroll=4))
    list_ref[last] = lax.div(count, BATCH)
    count = padded(lax.fori_loop(0, places, into, count, unroll=4))
    list_ref[last + 1] = lax.div(count, BATCH)


def spread_kernel(turned, n_pieces, *refs):
    if turned:
        info_ref, list_ref, base_out_ref, base_in_ref, own_ref, w_a_ref, w_b_ref, w_c_ref, away_ref = refs[:9]
        refs = refs[9:]
    else:
        info_ref, sent_ref, base_out_ref, base_in_ref, arrived_ref, away_ref = refs[:6]
        refs = refs[6:]
    landed_refs, piece_refs, refs = refs[:8], refs[8 : 8 + n_pieces], refs[8 + n_pieces :]
    if turned:
        total_ref, p1a_ref, p1b_ref, p2a_ref, p2b_ref, p3a_ref, p3b_ref = refs[:7]
        acc, every, tiles, landed, piece_sems, tile_sem, landed_sems, weights = refs[7:]
    else:
        out_ref, in_ref, list_ref = refs[:3]
        acc, every, tiles, landed, piece_sems, tile_sem, landed_sems, arrived, codes, got, code_sems = refs[3:]
    side = every.shape[1]
    blocks = base_out_ref.shape[0] // side
    plane = info_ref[2]
    planes, places = landed.shape[0], landed.shape[1]
    half, middle = blocks // 2, places // 2
    last = list_ref.shape[0] - 2
    starts = [pltpu.make_async_copy(away_ref, tiles, tile_sem.at[0])]
    for index, ref in enumerate(landed_refs):
        home = landed.at[jnp.bitwise_and(plane + (0, 0, -1, -1, 1, 1, 2, 2)[index], planes - 1), pl.ds((index % 2) * middle, middle)]
        starts.append(pltpu.make_async_copy(ref, home, landed_sems.at[index]))
    offset = 0
    for index, ref in enumerate(piece_refs):
        starts.append(pltpu.make_async_copy(ref, every.at[pl.ds(offset, ref.shape[0])], piece_sems.at[index]))
        offset += ref.shape[0]
    if not turned:
        rows = arrived_ref.shape[1] - CODES
        fetch = pltpu.make_async_copy(arrived_ref.at[:, pl.ds(rows, CODES), :], arrived, code_sems.at[0])
        fetch.start()
    for copy in starts:
        copy.start()
    if not turned:
        fetch.wait()
        codes[...] = arrived[:, 0, :].astype(F32).astype(jnp.int32)
        store = pltpu.make_async_copy(codes, got, code_sems.at[1])
        store.start()

    def clear(row, carry):
        acc[row] = jnp.zeros(acc.shape[1:], F32)
        return carry

    lax.fori_loop(0, acc.shape[0], clear, 0)
    if turned:
        for kind, ref in enumerate((w_a_ref, w_b_ref, w_c_ref)):
            for step in range(planes):
                at = pl.ds(pl.multiple_of(jnp.bitwise_and(plane + step, planes - 1) * side, side), side)
                weights[kind, step * side : (step + 1) * side, :] = ref[at, :]
    else:
        store.wait()
        list_products(info_ref, sent_ref, got, list_ref, blocks)
    for copy in starts:
        copy.wait()

    def batches(first_batch, end_batch, tile_of):
        def add_batch(batch, carry):
            codes = [list_ref[batch * BATCH + index] for index in range(BATCH)]
            products = [
                jnp.dot(
                    tile_of(jnp.bitwise_and(jnp.right_shift(code, 5), 63)),
                    every[jnp.right_shift(code, 11)],
                    preferred_element_type=F32,
                )
                for code in codes
            ]
            for code, product in zip(codes, products):
                row = jnp.bitwise_and(code, 31)
                acc[row] = acc[row] + product
            return carry

        lax.fori_loop(first_batch, end_batch, add_batch, 0)

    batches(0, list_ref[last], lambda place: tiles[place])
    batches(list_ref[last], list_ref[last + 1], lambda place: jnp.concatenate([landed[index, place] for index in range(planes)], axis=0))

    def sums(block):
        at = pl.ds(pl.multiple_of(block * side, side), side)
        return (acc[block] + base_out_ref[at, :]).astype(BF16), (acc[blocks + block] + base_in_ref[at, :]).astype(BF16), at

    def times(values, kind):
        return lax.dot_general(values, weights[kind], (((1,), (1,)), ((), ())), preferred_element_type=F32)

    def keep(block, carry):
        out, into, at = sums(block)
        out_ref[at, :] = out
        in_ref[at, :] = into
        return carry

    def multiply(low):
        def at_block(block, carry):
            out, into, at = sums(block)
            to = pl.ds(pl.multiple_of((block - low) * side, side), side)
            part = (times(out, 0) + times(into, 1)) * (1.0 / 32.0) + times(own_ref[at, :], 2)
            total_ref[at, :] = part[:, :side]
            for index, ref in enumerate((p1a_ref, p2a_ref, p3a_ref) if low == 0 else (p1b_ref, p2b_ref, p3b_ref)):
                ref[to, :] = part[:, (index + 1) * side : (index + 2) * side].astype(ref.dtype)
            return carry

        return at_block

    if turned:
        lax.fori_loop(0, half, multiply(0), 0)
        lax.fori_loop(half, blocks, multiply(half), 0)
    else:
        lax.fori_loop(0, blocks, keep, 0)


def spread(info, listing, base_out, base_in, others, away, landed, pieces, turned):
    side, places = away.shape[1], away.shape[0]
    rows, width = base_out.shape
    blocks = rows // side
    planes = side * CAP // landed[0].shape[1]
    every = sum(piece.shape[0] for piece in pieces) // side
    vmem = pl.BlockSpec(memory_space=pltpu.VMEM)
    smem = pl.BlockSpec(memory_space=pltpu.SMEM)
    far = pl.BlockSpec(memory_space=pltpu.HBM)
    landed = [piece.reshape(-1, side // planes, side) for piece in landed]
    pieces = [piece.reshape(-1, side, width) for piece in pieces]

    def shape(count, kind):
        return jax.ShapeDtypeStruct((count, width), kind)

    devices = places // CAP
    scratch = [
        pltpu.VMEM((2 * blocks + 1, side, width), F32),
        pltpu.VMEM((every, side, width), BF16),
        pltpu.VMEM((places, side, side), BF16),
        pltpu.VMEM((planes, places, side // planes, side), BF16),
        pltpu.SemaphoreType.DMA((len(pieces),)),
        pltpu.SemaphoreType.DMA((1,)),
        pltpu.SemaphoreType.DMA((len(landed),)),
    ]
    if turned:
        out_shape = [shape(rows, F32)] + [shape(rows // 2, kind) for kind in (F32, BF16, BF16, BF16, BF16, F32)]
        out_specs = [vmem] * len(out_shape)
        scratch += [pltpu.VMEM((3, planes * width, width), BF16)]
        other_specs = [vmem] * len(others)
    else:
        out_shape = [shape(rows, BF16), shape(rows, BF16), jax.ShapeDtypeStruct((2 * (places + BATCH) + 2,), jnp.int32)]
        out_specs = [vmem, vmem, smem]
        scratch += [
            pltpu.VMEM((devices, CODES, side), BF16),
            pltpu.VMEM((devices, side), jnp.int32),
            pltpu.SMEM((devices, side), jnp.int32),
            pltpu.SemaphoreType.DMA((2,)),
        ]
        other_specs = [far]
    return pl.pallas_call(
        lambda *refs: spread_kernel(turned, len(pieces), *refs),
        in_specs=[smem] * 2 + [vmem] * 2 + other_specs + [far] * (1 + len(landed) + len(pieces)),
        out_specs=out_specs,
        out_shape=out_shape,
        scratch_shapes=scratch,
        compiler_params=pltpu.CompilerParams(vmem_limit_bytes=ROOM),
        cost_estimate=pl.CostEstimate(flops=2 * rows * width * 3 * 512 + places * side**3 * 2, bytes_accessed=16 * MIB, transcendentals=0),
        name="spread",
    )(info, listing, base_out, base_in, *others, away, *landed, *pieces)


def activate_kernel(info_ref, *refs):
    planes = 4
    sides, weight_refs, refs = refs[: 3 * planes], refs[3 * planes : 3 * planes + 3], refs[3 * planes + 3 :]
    cotangent_ref, hidden_ref, grad_ref, weights = refs
    rows, width = cotangent_ref.shape
    plane = info_ref[2]
    for kind, ref in enumerate(weight_refs):
        for index, step in enumerate((0, -1, 1, 2)):
            at = pl.ds(pl.multiple_of(jnp.bitwise_and(plane + step, planes - 1) * width, width), width)
            weights[kind, index * width : (index + 1) * width, :] = ref[at, :]
    tall = 256

    def rows_at(turn, carry):
        at = pl.ds(pl.multiple_of(turn * tall, tall), tall)

        def times(kind):
            values = jnp.concatenate([ref[at, :] for ref in sides[kind * planes : (kind + 1) * planes]], axis=1)
            return jnp.dot(values, weights[kind], preferred_element_type=F32)

        value = (times(0) + times(1)) * (1.0 / 32.0) + times(2)
        gate = 1.0 / (1.0 + jnp.exp(-value))
        hidden_ref[at, :] = (value * gate).astype(BF16)
        grad_ref[at, :] = (cotangent_ref[at, :].astype(F32) * gate * (1.0 + value * (1.0 - gate))).astype(BF16)
        return carry

    lax.fori_loop(0, rows // tall, rows_at, 0)


def activate(info, outs, ins, selves, weights, cotangent):
    rows, width = cotangent.shape
    vmem = pl.BlockSpec(memory_space=pltpu.VMEM)
    return pl.pallas_call(
        activate_kernel,
        in_specs=[pl.BlockSpec(memory_space=pltpu.SMEM)] + [vmem] * 16,
        out_specs=[vmem] * 2,
        out_shape=[jax.ShapeDtypeStruct((rows, width), BF16)] * 2,
        scratch_shapes=[pltpu.VMEM((3, 4 * width, width), BF16)],
        compiler_params=pltpu.CompilerParams(vmem_limit_bytes=ROOM),
        cost_estimate=pl.CostEstimate(flops=2 * rows * 3 * 512 * width, bytes_accessed=4 * MIB, transcendentals=rows * width),
        name="activate",
    )(info, *outs, *ins, *selves, *weights, cotangent)


def slopes_kernel(info_ref, *refs):
    planes = 4
    grad_ref, out_ref, left = refs[3 * planes :]
    width = grad_ref.shape[1]
    slivers = out_ref.shape[1] // 3
    strips = width // slivers
    plane = info_ref[2]
    for kind in range(3):
        for index in range(planes):
            left[:, index * width : (index + 1) * width] = refs[kind * planes + index][...]
        terms = lax.dot_general(grad_ref[...], left[...], (((0,), (0,)), ((), ())), preferred_element_type=F32)
        for index, step in enumerate((0, -1, 1, 2)):
            first = jnp.bitwise_and(plane + step, planes - 1) * strips
            turned = terms[:, index * width : (index + 1) * width].T
            for strip in range(strips):
                out_ref[first + strip, kind * slivers : (kind + 1) * slivers, :] = turned[strip * slivers : (strip + 1) * slivers, :]


def slopes(info, outs, ins, selves, grad_z, devices):
    rows, width = grad_z.shape
    vmem = pl.BlockSpec(memory_space=pltpu.VMEM)
    return pl.pallas_call(
        slopes_kernel,
        in_specs=[pl.BlockSpec(memory_space=pltpu.SMEM)] + [vmem] * 13,
        out_specs=vmem,
        out_shape=jax.ShapeDtypeStruct((devices, 3 * width * 4 // devices, width), F32),
        scratch_shapes=[pltpu.VMEM((rows, 4 * width), BF16)],
        compiler_params=pltpu.CompilerParams(vmem_limit_bytes=ROOM),
        cost_estimate=pl.CostEstimate(flops=2 * rows * 3 * width * 4 * width, bytes_accessed=4 * MIB, transcendentals=0),
        name="slopes",
    )(info, *outs, *ins, *selves, grad_z)


def around(devices, stage, step):
    pairs = []
    for here in range(devices):
        core, x, y = here % 2, here // 2 % 4, here // 8
        if (core + stage) % 2 == 0:
            x = (x + step) % 4
        else:
            y = (y + step) % 4
        pairs.append((here, (y * 4 + x) * 2 + core))
    return pairs


def gather(values, devices, core, ahead):
    half = values.shape[0] // 2

    def forward(part, stage):
        return lax.ppermute(part, "nodes", around(devices, stage, 1))

    def backward(part, stage):
        return lax.ppermute(part, "nodes", around(devices, stage, -1))

    def sister(part):
        return lax.ppermute(part, "nodes", [(here, here ^ 1) for here in range(devices)])

    kept = lax.dynamic_slice_in_dim(values, core * half, half, 0)
    given = lax.dynamic_slice_in_dim(values, (1 - core) * half, half, 0)
    zero = jnp.concatenate([kept, sister(given)])
    if ahead is not None:
        zero, ahead = lax.optimization_barrier((zero, ahead))
    plus, minus = forward(zero, 0), backward(zero, 0)
    plus_far, minus_far = forward(plus[:half], 0), backward(minus[half:], 0)
    low = jnp.concatenate([zero, plus])
    high = jnp.concatenate([plus_far, minus_far, minus])
    plus_low, minus_low = forward(low, 1), backward(low, 1)
    plus_high, minus_high = forward(high, 1), backward(high, 1)
    plus_far, minus_far = forward(plus_low, 1), backward(minus_high, 1)
    own = [low, high, plus_low, plus_high, plus_far, minus_far, minus_low, minus_high]
    return own + [sister(piece) for piece in own], ahead, high


def shards(
    node_features, w_out, w_in, w_self, cotangent, tile_src, tile_dst, tile_pattern, tile_count
):
    devices = lax.axis_size("nodes")
    planes = lax.axis_size("hid")
    myself = lax.axis_index("nodes").astype(jnp.int32)
    plane = lax.axis_index("hid").astype(jnp.int32)
    core = lax.rem(myself, 2)
    side = tile_pattern.shape[1]
    rows, width = node_features.shape
    blocks = rows // side
    halves = rows // 2
    middle = devices // 2

    def shift(values, step):
        return lax.ppermute(values, "hid", [(here, (here + step) % planes) for here in range(planes)])

    def all_columns(part):
        left, right = shift(part, 1), shift(part, -1)
        return [part, left, right, shift(part, 2)]

    info = jnp.stack([tile_count[0], myself, plane, lax.rem(lax.div(myself, 2), 4), lax.div(myself, 8), core])
    away, send, sent = pick(tile_src, tile_dst, info, tile_pattern, blocks, devices, planes)
    pieces_x, (send, later_x), high = gather(node_features, devices, core, (send, node_features))
    arrived = lax.all_to_all(send, "nodes", 0, 0, tiled=True)
    part = send.shape[1] - CODES
    own_a, own_b = arrived[:middle, :part, :], arrived[middle:, :part, :]
    left_a, right_b = shift(own_a, 1), shift(own_b, -1)
    left_b, right_a = shift(own_b, 1), shift(own_a, -1)
    landed = [own_a, own_b, left_a, left_b, right_a, right_b, shift(left_a, 1), shift(right_b, -1)]
    pile_info, later_x, _ = lax.optimization_barrier((info, later_x, high))
    local = pile(tile_src, tile_dst, pile_info, tile_pattern, blocks)
    all_x = all_columns(later_x)

    def local_sums(values):
        return (
            jnp.dot(local, values, preferred_element_type=F32),
            jnp.einsum("ij,ik->jk", local, values, preferred_element_type=F32),
        )

    def collect(own, p1a, p1b, p2a, p2b, p3a, p3b):
        left, right = shift(p2a, 1), shift(p2b, -1)
        one_b, three_a = shift(p1b, 1), shift(p3a, -1)
        one_a = shift((p1a + left.astype(F32)).astype(BF16), 1)
        three_b = shift((p3b + right.astype(F32)).astype(BF16), -1)
        low = own[:halves] + one_a.astype(F32) + three_a.astype(F32)
        high = own[halves:] + one_b.astype(F32) + three_b.astype(F32)
        return jnp.concatenate([low, high])

    base_out, base_in = local_sums(node_features)
    prop_out, prop_in, listed = spread(info, sent, base_out, base_in, [arrived], away, landed, pieces_x, False)
    out_left, in_right = shift(prop_out, 1), shift(prop_in, -1)
    in_left, out_right = shift(prop_in, 1), shift(prop_out, -1)
    all_out = [prop_out, out_left, out_right, shift(out_left, 1)]
    all_in = [prop_in, in_left, in_right, shift(in_right, -1)]
    weights = [w_out, w_in, w_self]
    hidden, grad_z = activate(info, all_out, all_in, all_x, weights, cotangent)

    terms = slopes(info, all_out, all_in, all_x, grad_z, devices)
    pieces_z, terms, high = gather(grad_z, devices, core, terms)
    terms, _ = lax.optimization_barrier((terms, high))
    base_out, base_in = local_sums(grad_z)
    parts = spread(info, listed, base_out, base_in, [grad_z, w_in, w_out, w_self], away, landed, pieces_z, True)
    grad_input = collect(*parts).astype(BF16)

    slivers = width * planes // devices
    grads = jnp.sum(lax.all_to_all(terms, "nodes", 0, 0, tiled=True), axis=0).reshape(3, slivers, width)
    return (hidden, grad_input, grads[0] / 32.0, grads[1] / 32.0, grads[2])


def solution(mesh):
    in_specs = (
        P("nodes", "hid"),
        P(None, "hid"),
        P(None, "hid"),
        P(None, "hid"),
        P("nodes", "hid"),
        P("nodes"),
        P("nodes"),
        P("nodes", None, None),
        P("nodes"),
    )
    out_specs = (
        P("nodes", "hid"),
        P("nodes", "hid"),
        P("nodes", "hid"),
        P("nodes", "hid"),
        P("nodes", "hid"),
    )
    return jax.shard_map(shards, mesh=mesh, in_specs=in_specs, out_specs=out_specs, check_vma=False)
```

```python
import jax
import jax.numpy as jnp
from jax import lax
from jax.experimental import pallas as pl
from jax.experimental.pallas import tpu as pltpu
from jax.sharding import PartitionSpec as P

CAP = 2
GROUP = 16
BATCH = 8
CODES = 16
PICKS = 4
MIB = 1024 * 1024
ROOM = 63 * MIB
LESS = 16 * MIB
F32 = jnp.float32
BF16 = jnp.bfloat16


def split(value, size):
    shift = size.bit_length() - 1
    return jnp.right_shift(value, shift), jnp.bitwise_and(value, size - 1)


def pick_kernel(blocks, src_ref, dst_ref, info_ref, pattern_ref, away_ref, send_ref, meta_ref, tiles, counts, listed, sems):
    side = tiles.shape[1]
    devices = counts.shape[0]
    part = (send_ref.shape[1] - CODES) // CAP
    total, myself, first_row = info_ref[0], info_ref[1], jnp.bitwise_and(info_ref[2], 1) * part

    def clear(owner, carry):
        counts[owner] = 0
        for rank in range(CAP):
            meta_ref[owner * CAP + rank] = 0
        return carry

    lax.fori_loop(0, devices, clear, 0, unroll=4)

    def copy(slot, entry):
        return pltpu.make_async_copy(pattern_ref.at[slot], tiles.at[entry], sems.at[entry])

    def scan(slot, found):
        owner, _ = split(dst_ref[slot], blocks)
        listed[found] = slot
        return found + ((owner != myself) & (slot < total)).astype(jnp.int32)

    found = lax.fori_loop(0, dst_ref.shape[0], scan, 0, unroll=8)
    found = jnp.minimum(found, devices * CAP)

    def keep(entry, carry):
        slot = listed[entry]
        copy(slot, entry).start()
        owner, landing = split(dst_ref[slot], blocks)
        source = jnp.clip(src_ref[slot] - myself * blocks, 0, blocks - 1)
        rank = jnp.minimum(counts[owner], CAP - 1)
        counts[owner] = rank + 1
        place = owner * CAP + rank
        meta_ref[place] = 1 + source + blocks * landing
        listed[entry] = place
        return carry

    lax.fori_loop(0, found, keep, 0)
    row = lax.broadcasted_iota(jnp.int32, (part, side), 0)
    column = lax.broadcasted_iota(jnp.int32, (part, side), 1)
    chosen = (column == row + first_row).astype(F32).astype(BF16)

    def turn(batch, carry):
        first = batch * PICKS
        for index in range(PICKS):

            @pl.when(first + index < found)
            def arrive():
                copy(0, first + index).wait()

        entries = [jnp.minimum(first + index, found - 1) for index in range(PICKS)]
        values = [tiles[entry].astype(F32).astype(BF16) for entry in entries]
        turned = [
            lax.dot_general(chosen, value, (((1,), (1,)), ((), ())), preferred_element_type=F32).astype(BF16) for value in values
        ]
        for index, entry in enumerate(entries):
            place = listed[entry]
            owner, rank = split(place, CAP)
            away_ref[place] = values[index]
            send_ref[owner, pl.ds(pl.multiple_of(rank * part, part), part), :] = turned[index]
        return carry

    lax.fori_loop(0, lax.div(found + PICKS - 1, PICKS), turn, 0)
    lane = lax.broadcasted_iota(jnp.int32, (CODES, side), 1)

    def code(owner, carry):
        values = jnp.zeros((CODES, side), jnp.int32)
        for rank in range(CAP):
            values = jnp.where(lane == rank, meta_ref[owner * CAP + rank], values)
        send_ref[owner, CAP * part :, :] = values.astype(F32).astype(BF16)
        return carry

    lax.fori_loop(0, devices, code, 0, unroll=4)


def pick(tile_src, tile_dst, info, tile_pattern, blocks, devices):
    side = tile_pattern.shape[1]
    places = devices * CAP
    vmem = pl.BlockSpec(memory_space=pltpu.VMEM)
    smem = pl.BlockSpec(memory_space=pltpu.SMEM)
    return pl.pallas_call(
        lambda *refs: pick_kernel(blocks, *refs),
        in_specs=[smem, smem, smem, pl.BlockSpec(memory_space=pltpu.HBM)],
        out_specs=[vmem, vmem, smem],
        out_shape=[
            jax.ShapeDtypeStruct((places, side, side), BF16),
            jax.ShapeDtypeStruct((devices, CAP * side // 2 + CODES, side), BF16),
            jax.ShapeDtypeStruct((places,), jnp.int32),
        ],
        scratch_shapes=[
            pltpu.VMEM((places, side, side), jnp.int32),
            pltpu.SMEM((devices,), jnp.int32),
            pltpu.SMEM((tile_src.shape[0] + 1,), jnp.int32),
            pltpu.SemaphoreType.DMA((places,)),
        ],
        compiler_params=pltpu.CompilerParams(vmem_limit_bytes=ROOM),
        cost_estimate=pl.CostEstimate(flops=places * side * side, bytes_accessed=8 * MIB, transcendentals=0),
        name="pick",
    )(tile_src, tile_dst, info, tile_pattern)


def own_products(local_ref, values_ref, out_ref, in_ref):
    side = values_ref.shape[1]

    def block(index, carry):
        at = pl.ds(pl.multiple_of(index * side, side), side)
        out_ref[at, :] = jnp.dot(local_ref[at, :], values_ref[...], preferred_element_type=F32)
        return carry

    lax.fori_loop(0, values_ref.shape[0] // side, block, 0)
    for index in range(values_ref.shape[0] // side):
        span = slice(index * side, (index + 1) * side)
        in_ref[span, :] = lax.dot_general(local_ref[:, span], values_ref[...], (((0,), (0,)), ((), ())), preferred_element_type=F32)


def pile_kernel(src_ref, dst_ref, info_ref, pattern_ref, values_ref, local_ref, out_ref, in_ref, acc, groups, sems):
    depth, group, side = groups.shape[0], groups.shape[1], groups.shape[2]
    blocks = local_ref.shape[0] // side
    total, myself = info_ref[0], info_ref[1]
    turns = lax.div(total + group - 1, group)

    def copy(turn):
        return pltpu.make_async_copy(pattern_ref.at[pl.ds(turn * group, group)], groups.at[turn], sems.at[turn])

    for turn in range(depth):

        @pl.when(turn < turns)
        def begin():
            copy(turn).start()

    def clear(pair, carry):
        acc[pair] = jnp.zeros((side, side), jnp.int32)
        return carry

    lax.fori_loop(0, acc.shape[0], clear, 0)

    def take(turn, carry):
        copy(turn).wait()

        def add(index, carry):
            slot = turn * group + index
            source = jnp.clip(src_ref[slot] - myself * blocks, 0, blocks - 1)
            owner, landing = split(dst_ref[slot], blocks)
            pair = jnp.where((owner == myself) & (slot < total), source * blocks + landing, blocks * blocks)
            acc[pair] = acc[pair] + groups[turn, index]
            return carry

        lax.fori_loop(0, group, add, 0, unroll=4)
        return carry

    lax.fori_loop(0, turns, take, 0)

    def finish(source, carry):
        rows = pl.ds(pl.multiple_of(source * side, side), side)
        for landing in range(blocks):
            local_ref[rows, landing * side : (landing + 1) * side] = acc[source * blocks + landing].astype(F32).astype(BF16)
        return carry

    lax.fori_loop(0, blocks, finish, 0)
    own_products(local_ref, values_ref, out_ref, in_ref)


def pile(tile_src, tile_dst, info, tile_pattern, values):
    slots, side = tile_pattern.shape[0], tile_pattern.shape[1]
    blocks = values.shape[0] // side
    smem = pl.BlockSpec(memory_space=pltpu.SMEM)
    vmem = pl.BlockSpec(memory_space=pltpu.VMEM)
    return pl.pallas_call(
        pile_kernel,
        in_specs=[smem, smem, smem, pl.BlockSpec(memory_space=pltpu.HBM), vmem],
        out_specs=[vmem] * 3,
        out_shape=[jax.ShapeDtypeStruct((blocks * side, blocks * side), BF16)] + [jax.ShapeDtypeStruct(values.shape, F32)] * 2,
        scratch_shapes=[
            pltpu.VMEM((blocks * blocks + 1, side, side), jnp.int32),
            pltpu.VMEM((slots // GROUP, GROUP, side, side), jnp.int32),
            pltpu.SemaphoreType.DMA((slots // GROUP,)),
        ],
        compiler_params=pltpu.CompilerParams(vmem_limit_bytes=ROOM),
        cost_estimate=pl.CostEstimate(flops=slots * side * side, bytes_accessed=slots * side * side * 4, transcendentals=0),
        name="pile",
    )(tile_src, tile_dst, info, tile_pattern, values)


def list_products(info_ref, sent_ref, got_ref, list_ref, blocks):
    x, y, core = info_ref[3], info_ref[4], info_ref[5]
    places = sent_ref.shape[0]
    last = list_ref.shape[0] - 2

    def entry(device, block, place, row):
        chip, their_core = split(device, 2)
        their_y, their_x = split(chip, 4)
        step_x, step_y = jnp.bitwise_and(x - their_x, 3), jnp.bitwise_and(y - their_y, 3)
        first = jnp.where(their_core == 0, step_x, step_y)
        second = jnp.where(their_core == 0, step_y, step_x)
        index = (second * 4 + first) * blocks + block + jnp.where(their_core == core, 0, 16 * blocks)
        return (index * 64 + place) * 32 + row

    def out(place, count):
        code = sent_ref[place] - 1
        landing, source = split(jnp.maximum(code, 0), blocks)
        list_ref[count] = entry(jnp.right_shift(place, 1), landing, place, source)
        return count + (code >= 0).astype(jnp.int32)

    def into(place, count):
        code = got_ref[jnp.right_shift(place, 1), jnp.bitwise_and(place, 1)] - 1
        landing, source = split(jnp.maximum(code, 0), blocks)
        list_ref[count] = entry(jnp.right_shift(place, 1), source, place, blocks + landing)
        return count + (code >= 0).astype(jnp.int32)

    def padded(count):
        ends = lax.div(count + BATCH - 1, BATCH) * BATCH

        def pad(index, carry):
            list_ref[index] = 2 * blocks
            return carry

        lax.fori_loop(count, ends, pad, 0)
        return ends

    count = padded(lax.fori_loop(0, places, out, 0, unroll=4))
    list_ref[last] = lax.div(count, BATCH)
    count = padded(lax.fori_loop(0, places, into, count, unroll=4))
    list_ref[last + 1] = lax.div(count, BATCH)


def spread_kernel(turned, n_pieces, *refs):
    info_ref, listing_ref, refs = refs[0], refs[1], refs[2:]
    n_loads, n_stores = (6, 7) if turned else (7, 9)
    load_refs, refs = refs[:n_loads], refs[n_loads:]
    (arrived_ref, other_a_ref, other_b_ref, away_ref), refs = refs[:4], refs[4:]
    piece_refs, store_refs, refs = refs[:n_pieces], refs[n_pieces : n_pieces + n_stores], refs[n_pieces + n_stores :]
    if turned:
        list_ref = listing_ref
    else:
        list_ref, refs = refs[0], refs[1:]
    loads, refs = refs[:n_loads], refs[n_loads:]
    stores, refs = refs[:n_stores], refs[n_stores:]
    acc, every, tiles, weights, piece_sems, tile_sems, load_sems, store_sems = refs[:8]
    refs = refs[8:]
    base_out, base_in = loads[:2]
    side = every.shape[1]
    blocks = base_out.shape[0] // side
    plane = info_ref[2]
    planes = 4
    half, part, devices = blocks // 2, side // 2, other_a_ref.shape[0]
    last = list_ref.shape[0] - 2
    if not turned:
        arrived, codes, got, code_sems = refs
        fetch = pltpu.make_async_copy(arrived_ref.at[:, pl.ds(CAP * part, CODES), :], arrived, code_sems.at[0])
        fetch.start()
    starts = []
    offset = 0
    for index, ref in enumerate(piece_refs):
        starts.append(pltpu.make_async_copy(ref, every.at[pl.ds(offset, ref.shape[0])], piece_sems.at[index]))
        offset += ref.shape[0]
    for copy in starts:
        copy.start(priority=1)
    fetched = [pltpu.make_async_copy(ref, to, load_sems.at[index]) for index, (ref, to) in enumerate(zip(load_refs, loads))]
    for copy in fetched:
        copy.start()
    if not turned:
        fetch.wait()
        codes[...] = arrived[:, 0, :].astype(F32).astype(jnp.int32)
        store = pltpu.make_async_copy(codes, got, code_sems.at[1])
        store.start()

    def clear(row, carry):
        acc[row] = jnp.zeros(acc.shape[1:], F32)
        return carry

    if not turned:
        lax.fori_loop(0, acc.shape[0], clear, 0)
        store.wait()
        list_products(info_ref, listing_ref, got, list_ref, blocks)

    def begin_away(index, carry):
        place = jnp.bitwise_and(jnp.right_shift(list_ref[index], 5), 63)
        pltpu.make_async_copy(away_ref.at[place], tiles.at[index], tile_sems.at[index]).start()
        return carry

    def begin_arrived(index, carry):
        device, rank = split(jnp.bitwise_and(jnp.right_shift(list_ref[index], 5), 63), CAP)
        rows = pl.ds(pl.multiple_of(rank * part, part), part)
        parity = jnp.bitwise_and(plane, 1)

        def bring(ref, at, step):
            to = tiles.at[index, pl.ds(pl.multiple_of(step * part, part), part), :]
            pltpu.make_async_copy(ref.at[at, rows, :], to, tile_sems.at[index]).start()

        bring(arrived_ref, device, parity)

        @pl.when(device < devices)
        def first():
            bring(other_a_ref, device, 1 - parity)

        @pl.when(device >= devices)
        def second():
            bring(other_b_ref, device - devices, 1 - parity)

        return carry

    middle, end = list_ref[last], list_ref[last + 1]
    lax.fori_loop(0, middle * BATCH, begin_away, 0)
    lax.fori_loop(middle * BATCH, end * BATCH, begin_arrived, 0)
    if turned:
        lax.fori_loop(0, acc.shape[0], clear, 0)
    for copy in fetched:
        copy.wait()
    for kind in range(3):
        for step in range(planes):
            span = slice(step * side, (step + 1) * side)
            if turned:
                at = pl.ds(pl.multiple_of(jnp.bitwise_and(plane + step, planes - 1) * side, side), side)
                weights[kind, span, :] = loads[3 + kind][at, :]
            else:
                weights[kind, :, span] = loads[3 + step][kind * side : (kind + 1) * side, :]
    for copy in starts:
        copy.wait()

    def add_batch(batch, carry):
        indices = [batch * BATCH + index for index in range(BATCH)]
        codes = [list_ref[index] for index in indices]
        for index in indices:
            pltpu.make_async_copy(away_ref.at[0], tiles.at[index], tile_sems.at[index]).wait()
        products = [
            jnp.dot(tiles[index], every[jnp.right_shift(code, 11)], preferred_element_type=F32) for index, code in zip(indices, codes)
        ]
        for code, product in zip(codes, products):
            row = jnp.bitwise_and(code, 31)
            acc[row] = acc[row] + product
        return carry

    lax.fori_loop(0, end, add_batch, 0)

    def sums(block):
        at = pl.ds(pl.multiple_of(block * side, side), side)
        return (acc[block] + base_out[at, :]).astype(BF16), (acc[blocks + block] + base_in[at, :]).astype(BF16), at

    def times(values, kind):
        return lax.dot_general(values, weights[kind], (((1,), (1 if turned else 0,)), ((), ())), preferred_element_type=F32)

    def multiply(low):
        def at_block(block, carry):
            out, into, at = sums(block)
            to = pl.ds(pl.multiple_of((block - low) * side, side), side)
            if not turned:
                stores[7][at, :] = out
                stores[8][at, :] = into
            part = (times(out, 0) + times(into, 1)) * (1.0 / 32.0) + times(loads[2][at, :], 2)
            stores[0][at, :] = part[:, :side]
            for index in range(3):
                ref = stores[1 + 2 * index + (low > 0)]
                ref[to, :] = part[:, (index + 1) * side : (index + 2) * side].astype(ref.dtype)
            return carry

        return at_block

    written = [pltpu.make_async_copy(ref, to, store_sems.at[index]) for index, (ref, to) in enumerate(zip(stores, store_refs))]
    lax.fori_loop(0, half, multiply(0), 0)
    for index in (3, 1, 5):
        written[index].start()
    lax.fori_loop(half, blocks, multiply(half), 0)
    for index in (4, 2, 6, 0) if turned else (4, 2, 6, 0, 7, 8):
        written[index].start()
    for copy in written:
        copy.wait()


def spread(info, listing, base_out, base_in, others, arrived, others_a_b, away, pieces, turned):
    side, places = away.shape[1], away.shape[0]
    rows, width = base_out.shape
    blocks = rows // side
    planes = 4
    entries = 2 * (places + BATCH)
    every = sum(piece.shape[0] for piece in pieces) // side
    smem = pl.BlockSpec(memory_space=pltpu.SMEM)
    far = pl.BlockSpec(memory_space=pltpu.HBM)
    pieces = [piece.reshape(-1, side, width) for piece in pieces]
    loads = [base_out, base_in, *others]

    def shape(count, kind):
        return jax.ShapeDtypeStruct((count, width), kind)

    devices = places // CAP
    out_shape = [shape(rows, F32)] + [shape(rows // 2, kind) for kind in (F32, BF16, BF16, BF16, BF16, F32)]
    if not turned:
        out_shape += [shape(rows, BF16), shape(rows, BF16)]
    scratch = [pltpu.VMEM(part.shape, part.dtype) for part in loads + out_shape]
    scratch += [
        pltpu.VMEM((2 * blocks + 1, side, width), F32),
        pltpu.VMEM((every, side, width), BF16),
        pltpu.VMEM((entries, side, side), BF16),
        pltpu.VMEM((3, planes * width, width) if turned else (3, width, planes * width), BF16),
        pltpu.SemaphoreType.DMA((len(pieces),)),
        pltpu.SemaphoreType.DMA((entries,)),
        pltpu.SemaphoreType.DMA((len(loads),)),
        pltpu.SemaphoreType.DMA((len(out_shape),)),
    ]
    out_specs = [far] * len(out_shape)
    if not turned:
        out_shape += [jax.ShapeDtypeStruct((entries + 2,), jnp.int32)]
        out_specs += [smem]
        scratch += [
            pltpu.VMEM((devices, CODES, side), BF16),
            pltpu.VMEM((devices, side), jnp.int32),
            pltpu.SMEM((devices, side), jnp.int32),
            pltpu.SemaphoreType.DMA((2,)),
        ]
    return pl.pallas_call(
        lambda *refs: spread_kernel(turned, len(pieces), *refs),
        in_specs=[smem] * 2 + [far] * (len(loads) + 4 + len(pieces)),
        out_specs=out_specs,
        out_shape=out_shape,
        scratch_shapes=scratch,
        compiler_params=pltpu.CompilerParams(vmem_limit_bytes=ROOM),
        cost_estimate=pl.CostEstimate(flops=2 * rows * width * 3 * 512 + places * side**3 * 2, bytes_accessed=16 * MIB, transcendentals=0),
        name="spread",
    )(info, listing, *loads, arrived, *others_a_b, away, *pieces)


def slopes_kernel(left_1_ref, left_2_ref, left_3_ref, z0_ref, z1_ref, z2_ref, z3_ref, out_ref, right):
    width = z0_ref.shape[1]
    planes = right.shape[1] // width
    strips = out_ref.shape[0] // planes
    slivers = out_ref.shape[1] // 3
    for step, ref in enumerate((z0_ref, z1_ref, z2_ref, z3_ref)):
        right[:, step * width : (step + 1) * width] = ref[...]
    for kind, ref in enumerate((left_1_ref, left_2_ref, left_3_ref)):
        terms = lax.dot_general(ref[...], right[...], (((0,), (0,)), ((), ())), preferred_element_type=F32)
        for step in range(planes):
            for strip in range(strips):
                out_ref[step * strips + strip, kind * slivers : (kind + 1) * slivers, :] = terms[
                    strip * slivers : (strip + 1) * slivers, step * width : (step + 1) * width
                ]


def slopes(lefts, rights, devices):
    rows, width = rights[0].shape
    vmem = pl.BlockSpec(memory_space=pltpu.VMEM)
    planes = len(rights)
    return pl.pallas_call(
        slopes_kernel,
        in_specs=[vmem] * 7,
        out_specs=vmem,
        out_shape=jax.ShapeDtypeStruct((devices, 3 * width * planes // devices, width), F32),
        scratch_shapes=[pltpu.VMEM((rows, planes * width), BF16)],
        compiler_params=pltpu.CompilerParams(vmem_limit_bytes=LESS),
        cost_estimate=pl.CostEstimate(flops=2 * rows * 3 * width * planes * width, bytes_accessed=3 * MIB, transcendentals=0),
        name="slopes",
    )(*lefts, *rights)


def around(devices, stage, step):
    pairs = []
    for here in range(devices):
        core, x, y = here % 2, here // 2 % 4, here // 8
        if (core + stage) % 2 == 0:
            x = (x + step) % 4
        else:
            y = (y + step) % 4
        pairs.append((here, (y * 4 + x) * 2 + core))
    return pairs


def sister(part, devices):
    return lax.ppermute(part, "nodes", [(here, here ^ 1) for here in range(devices)])


def gather(values, devices, before, between):
    def move(part, stage, step):
        return lax.ppermute(part, "nodes", around(devices, stage, step))

    plus, minus, far = move(values, 0, 1), move(values, 0, -1), move(values, 0, 2)
    row = jnp.concatenate([values, plus, far, minus])
    row, before = lax.optimization_barrier((row, before))
    plus, minus = move(row, 1, 1), move(row, 1, -1)
    plus, minus, between = lax.optimization_barrier((plus, minus, between(before)))
    half = row.shape[0] // 2
    plus_far, minus_far = move(plus[:half], 1, 1), move(minus[half:], 1, -1)
    own = [row, plus, plus_far, minus_far, minus]
    return own + [sister(piece, devices) for piece in own], before, between


def shards(
    node_features, w_out, w_in, w_self, cotangent, tile_src, tile_dst, tile_pattern, tile_count
):
    devices = lax.axis_size("nodes")
    planes = lax.axis_size("hid")
    myself = lax.axis_index("nodes").astype(jnp.int32)
    plane = lax.axis_index("hid").astype(jnp.int32)
    core = lax.rem(myself, 2)
    side = tile_pattern.shape[1]
    rows, width = node_features.shape
    blocks = rows // side
    halves = rows // 2

    def shift(values, step):
        return lax.ppermute(values, "hid", [(here, (here + step) % planes) for here in range(planes)])

    info = jnp.stack([tile_count[0], myself, plane, lax.rem(lax.div(myself, 2), 4), lax.div(myself, 8), core])
    away, send, sent = pick(tile_src, tile_dst, info, tile_pattern, blocks, devices)
    stacked = jnp.stack([w_out, w_in, w_self]).reshape(3, planes, width, width)

    def rows_of(step):
        return lax.dynamic_index_in_dim(stacked, (plane + step) % planes, 1, keepdims=False).reshape(3 * width, width)

    pieces_x, _, (local, base_out, base_in) = gather(
        node_features,
        devices,
        (info, node_features, send),
        lambda held: pile(tile_src, tile_dst, held[0], tile_pattern, held[1]),
    )
    forward = [rows_of(0)] + [shift(rows_of(-step), -step) for step in range(1, planes)]
    arrived = lax.all_to_all(send, "nodes", 0, 0, tiled=True)
    arrived, _ = lax.optimization_barrier((arrived, base_out))
    middle = devices // 2
    others = [
        lax.ppermute(arrived[:middle], "hid", [(here, here ^ 1) for here in range(planes)]),
        lax.ppermute(arrived[middle:], "hid", [(here, (here + 1 if here % 2 else here - 1) % planes) for here in range(planes)]),
    ]
    base_out, forward = lax.optimization_barrier((base_out, forward))

    def collect(own, p1a, p1b, p2a, p2b, p3a, p3b, give=False):
        left, right = shift(p2a, 1), shift(p2b, -1)
        one_b, three_a = shift(p1b, 1), shift(p3a, -1)
        one_a = shift((p1a + left.astype(F32)).astype(BF16), 1)
        three_b = shift((p3b + right.astype(F32)).astype(BF16), -1)
        low = own[:halves] + one_a.astype(F32) + three_a.astype(F32)
        high = own[halves:] + one_b.astype(F32) + three_b.astype(F32)
        return (jnp.concatenate([low, high]), (one_b, three_a)) if give else jnp.concatenate([low, high])

    *parts, prop_out, prop_in, listed = spread(
        info, sent, base_out, base_in, [node_features, *forward], arrived, others, away, pieces_x, False
    )
    pre_act = collect(*parts)
    hidden = jax.nn.silu(pre_act).astype(BF16)
    gate = jax.nn.sigmoid(pre_act)
    grad_z = (cotangent.astype(F32) * gate * (1.0 + pre_act * (1.0 - gate))).astype(BF16)

    rights = [grad_z] + [shift(grad_z, step) for step in range(1, planes)]
    base_out = jnp.dot(local, grad_z, preferred_element_type=F32)
    base_in = jnp.einsum("ij,ik->jk", local, grad_z, preferred_element_type=F32)
    slivers = width * planes // devices
    pieces_z, (base_out, base_in), terms = gather(
        grad_z, devices, (base_out, base_in), lambda held: slopes([prop_out, prop_in, node_features], rights, devices)
    )
    terms = lax.all_to_all(terms, "nodes", 0, 0, tiled=True)
    parts = spread(info, listed, base_out, base_in, [grad_z, w_in, w_out, w_self], arrived, others, away, pieces_z, True)
    grad_sum, middle_sum = collect(*parts, True)
    grad_input = grad_sum.astype(BF16)

    strips = width // slivers
    moves = [
        ((step * strips + strip) * planes + here, (here * strips + strip) * planes + (here - step) % planes)
        for step in range(planes)
        for strip in range(strips)
        for here in range(planes)
    ]
    summed, _ = lax.optimization_barrier((jnp.sum(terms, axis=0), middle_sum))
    grads = lax.ppermute(summed, ("nodes", "hid"), moves).reshape(3, slivers, width)
    return (hidden, grad_input, grads[0] / 32.0, grads[1] / 32.0, grads[2])


def solution(mesh):
    in_specs = (
        P("nodes", "hid"),
        P(None, "hid"),
        P(None, "hid"),
        P(None, "hid"),
        P("nodes", "hid"),
        P("nodes"),
        P("nodes"),
        P("nodes", None, None),
        P("nodes"),
    )
    out_specs = (
        P("nodes", "hid"),
        P("nodes", "hid"),
        P("nodes", "hid"),
        P("nodes", "hid"),
        P("nodes", "hid"),
    )
    return jax.shard_map(shards, mesh=mesh, in_specs=in_specs, out_specs=out_specs, check_vma=False)
```

```python
import jax
import jax.numpy as jnp
from jax import lax
from jax.experimental import pallas as pl
from jax.experimental.pallas import tpu as pltpu
from jax.sharding import PartitionSpec as P

CAP = 2
GROUP = 16
BATCH = 8
CODES = 16
PICKS = 4
MIB = 1024 * 1024
ROOM = 63 * MIB
LESS = 16 * MIB
F32 = jnp.float32
BF16 = jnp.bfloat16


def split(value, size):
    shift = size.bit_length() - 1
    return jnp.right_shift(value, shift), jnp.bitwise_and(value, size - 1)


def pick_kernel(blocks, src_ref, dst_ref, info_ref, pattern_ref, away_ref, send_ref, meta_ref, tiles, counts, listed, sems):
    side = tiles.shape[1]
    devices = counts.shape[0]
    part = (send_ref.shape[1] - CODES) // CAP
    total, myself, first_row = info_ref[0], info_ref[1], jnp.bitwise_and(info_ref[2], 1) * part

    def clear(owner, carry):
        counts[owner] = 0
        for rank in range(CAP):
            meta_ref[owner * CAP + rank] = 0
        return carry

    lax.fori_loop(0, devices, clear, 0, unroll=4)

    def copy(slot, entry):
        return pltpu.make_async_copy(pattern_ref.at[slot], tiles.at[entry], sems.at[entry])

    def scan(slot, found):
        owner, _ = split(dst_ref[slot], blocks)
        listed[found] = slot
        return found + ((owner != myself) & (slot < total)).astype(jnp.int32)

    found = lax.fori_loop(0, dst_ref.shape[0], scan, 0, unroll=8)
    found = jnp.minimum(found, devices * CAP)

    def keep(entry, carry):
        slot = listed[entry]
        copy(slot, entry).start()
        owner, landing = split(dst_ref[slot], blocks)
        source = jnp.clip(src_ref[slot] - myself * blocks, 0, blocks - 1)
        rank = jnp.minimum(counts[owner], CAP - 1)
        counts[owner] = rank + 1
        place = owner * CAP + rank
        meta_ref[place] = 1 + source + blocks * landing
        listed[entry] = place
        return carry

    lax.fori_loop(0, found, keep, 0)
    row = lax.broadcasted_iota(jnp.int32, (part, side), 0)
    column = lax.broadcasted_iota(jnp.int32, (part, side), 1)
    chosen = (column == row + first_row).astype(F32).astype(BF16)

    def turn(batch, carry):
        first = batch * PICKS
        for index in range(PICKS):

            @pl.when(first + index < found)
            def arrive():
                copy(0, first + index).wait()

        entries = [jnp.minimum(first + index, found - 1) for index in range(PICKS)]
        values = [tiles[entry].astype(F32).astype(BF16) for entry in entries]
        turned = [
            lax.dot_general(chosen, value, (((1,), (1,)), ((), ())), preferred_element_type=F32).astype(BF16) for value in values
        ]
        for index, entry in enumerate(entries):
            place = listed[entry]
            owner, rank = split(place, CAP)
            away_ref[place] = values[index]
            send_ref[owner, pl.ds(pl.multiple_of(rank * part, part), part), :] = turned[index]
        return carry

    lax.fori_loop(0, lax.div(found + PICKS - 1, PICKS), turn, 0)
    lane = lax.broadcasted_iota(jnp.int32, (CODES, side), 1)

    def code(owner, carry):
        values = jnp.zeros((CODES, side), jnp.int32)
        for rank in range(CAP):
            values = jnp.where(lane == rank, meta_ref[owner * CAP + rank], values)
        send_ref[owner, CAP * part :, :] = values.astype(F32).astype(BF16)
        return carry

    lax.fori_loop(0, devices, code, 0, unroll=4)


def pick(tile_src, tile_dst, info, tile_pattern, blocks, devices):
    side = tile_pattern.shape[1]
    places = devices * CAP
    vmem = pl.BlockSpec(memory_space=pltpu.VMEM)
    smem = pl.BlockSpec(memory_space=pltpu.SMEM)
    return pl.pallas_call(
        lambda *refs: pick_kernel(blocks, *refs),
        in_specs=[smem, smem, smem, pl.BlockSpec(memory_space=pltpu.HBM)],
        out_specs=[vmem, vmem, smem],
        out_shape=[
            jax.ShapeDtypeStruct((places, side, side), BF16),
            jax.ShapeDtypeStruct((devices, CAP * side // 2 + CODES, side), BF16),
            jax.ShapeDtypeStruct((places,), jnp.int32),
        ],
        scratch_shapes=[
            pltpu.VMEM((places, side, side), jnp.int32),
            pltpu.SMEM((devices,), jnp.int32),
            pltpu.SMEM((tile_src.shape[0] + 1,), jnp.int32),
            pltpu.SemaphoreType.DMA((places,)),
        ],
        compiler_params=pltpu.CompilerParams(vmem_limit_bytes=ROOM),
        cost_estimate=pl.CostEstimate(flops=places * side * side, bytes_accessed=8 * MIB, transcendentals=0),
        name="pick",
    )(tile_src, tile_dst, info, tile_pattern)


def own_products(local_ref, values_ref, out_ref, in_ref):
    side = values_ref.shape[1]

    def block(index, carry):
        at = pl.ds(pl.multiple_of(index * side, side), side)
        out_ref[at, :] = jnp.dot(local_ref[at, :], values_ref[...], preferred_element_type=F32)
        return carry

    lax.fori_loop(0, values_ref.shape[0] // side, block, 0)
    for index in range(values_ref.shape[0] // side):
        span = slice(index * side, (index + 1) * side)
        in_ref[span, :] = lax.dot_general(local_ref[:, span], values_ref[...], (((0,), (0,)), ((), ())), preferred_element_type=F32)


def pile_kernel(src_ref, dst_ref, info_ref, pattern_ref, values_ref, local_ref, out_ref, in_ref, acc, groups, sems):
    depth, group, side = groups.shape[0], groups.shape[1], groups.shape[2]
    blocks = local_ref.shape[0] // side
    total, myself = info_ref[0], info_ref[1]
    turns = lax.div(total + group - 1, group)

    def copy(turn):
        return pltpu.make_async_copy(pattern_ref.at[pl.ds(turn * group, group)], groups.at[turn], sems.at[turn])

    for turn in range(depth):

        @pl.when(turn < turns)
        def begin():
            copy(turn).start()

    def clear(pair, carry):
        acc[pair] = jnp.zeros((side, side), jnp.int32)
        return carry

    lax.fori_loop(0, acc.shape[0], clear, 0)

    def take(turn, carry):
        copy(turn).wait()

        def add(index, carry):
            slot = turn * group + index
            source = jnp.clip(src_ref[slot] - myself * blocks, 0, blocks - 1)
            owner, landing = split(dst_ref[slot], blocks)
            pair = jnp.where((owner == myself) & (slot < total), source * blocks + landing, blocks * blocks)
            acc[pair] = acc[pair] + groups[turn, index]
            return carry

        lax.fori_loop(0, group, add, 0, unroll=4)
        return carry

    lax.fori_loop(0, turns, take, 0)

    def finish(source, carry):
        rows = pl.ds(pl.multiple_of(source * side, side), side)
        for landing in range(blocks):
            local_ref[rows, landing * side : (landing + 1) * side] = acc[source * blocks + landing].astype(F32).astype(BF16)
        return carry

    lax.fori_loop(0, blocks, finish, 0)
    own_products(local_ref, values_ref, out_ref, in_ref)


def pile(tile_src, tile_dst, info, tile_pattern, values):
    slots, side = tile_pattern.shape[0], tile_pattern.shape[1]
    blocks = values.shape[0] // side
    smem = pl.BlockSpec(memory_space=pltpu.SMEM)
    vmem = pl.BlockSpec(memory_space=pltpu.VMEM)
    return pl.pallas_call(
        pile_kernel,
        in_specs=[smem, smem, smem, pl.BlockSpec(memory_space=pltpu.HBM), vmem],
        out_specs=[vmem] * 3,
        out_shape=[jax.ShapeDtypeStruct((blocks * side, blocks * side), BF16)] + [jax.ShapeDtypeStruct(values.shape, F32)] * 2,
        scratch_shapes=[
            pltpu.VMEM((blocks * blocks + 1, side, side), jnp.int32),
            pltpu.VMEM((slots // GROUP, GROUP, side, side), jnp.int32),
            pltpu.SemaphoreType.DMA((slots // GROUP,)),
        ],
        compiler_params=pltpu.CompilerParams(vmem_limit_bytes=ROOM),
        cost_estimate=pl.CostEstimate(flops=slots * side * side, bytes_accessed=slots * side * side * 4, transcendentals=0),
        name="pile",
    )(tile_src, tile_dst, info, tile_pattern, values)


def list_products(info_ref, sent_ref, got_ref, list_ref, blocks):
    x, y, core = info_ref[3], info_ref[4], info_ref[5]
    places = sent_ref.shape[0]
    last = list_ref.shape[0] - 2

    def entry(device, block, place, row):
        chip, their_core = split(device, 2)
        their_y, their_x = split(chip, 4)
        step_x, step_y = jnp.bitwise_and(x - their_x, 3), jnp.bitwise_and(y - their_y, 3)
        first = jnp.where(their_core == 0, step_x, step_y)
        second = jnp.where(their_core == 0, step_y, step_x)
        index = (second * 4 + first) * blocks + block + jnp.where(their_core == core, 0, 16 * blocks)
        return (index * 64 + place) * 32 + row

    def out(place, count):
        code = sent_ref[place] - 1
        landing, source = split(jnp.maximum(code, 0), blocks)
        list_ref[count] = entry(jnp.right_shift(place, 1), landing, place, source)
        return count + (code >= 0).astype(jnp.int32)

    def into(place, count):
        code = got_ref[jnp.right_shift(place, 1), jnp.bitwise_and(place, 1)] - 1
        landing, source = split(jnp.maximum(code, 0), blocks)
        list_ref[count] = entry(jnp.right_shift(place, 1), source, place, blocks + landing)
        return count + (code >= 0).astype(jnp.int32)

    def padded(count):
        ends = lax.div(count + BATCH - 1, BATCH) * BATCH

        def pad(index, carry):
            list_ref[index] = 2 * blocks
            return carry

        lax.fori_loop(count, ends, pad, 0)
        return ends

    count = padded(lax.fori_loop(0, places, out, 0, unroll=4))
    list_ref[last] = lax.div(count, BATCH)
    count = padded(lax.fori_loop(0, places, into, count, unroll=4))
    list_ref[last + 1] = lax.div(count, BATCH)


def spread_kernel(turned, n_pieces, *refs):
    info_ref, listing_ref, refs = refs[0], refs[1], refs[2:]
    n_loads, n_stores = (6, 7) if turned else (7, 9)
    load_refs, refs = refs[:n_loads], refs[n_loads:]
    (arrived_ref, other_a_ref, other_b_ref, away_ref), refs = refs[:4], refs[4:]
    piece_refs, store_refs, refs = refs[:n_pieces], refs[n_pieces : n_pieces + n_stores], refs[n_pieces + n_stores :]
    if turned:
        list_ref = listing_ref
    else:
        list_ref, refs = refs[0], refs[1:]
    loads, refs = refs[:n_loads], refs[n_loads:]
    stores, refs = refs[:n_stores], refs[n_stores:]
    acc, every, tiles, weights, piece_sems, tile_sems, load_sems, store_sems = refs[:8]
    refs = refs[8:]
    base_out, base_in = loads[:2]
    side = every.shape[1]
    blocks = base_out.shape[0] // side
    plane = info_ref[2]
    planes = 4
    half, part, devices = blocks // 2, side // 2, other_a_ref.shape[0]
    last = list_ref.shape[0] - 2
    if not turned:
        arrived, codes, got, code_sems = refs
        fetch = pltpu.make_async_copy(arrived_ref.at[:, pl.ds(CAP * part, CODES), :], arrived, code_sems.at[0])
        fetch.start()
    starts = []
    offset = 0
    for index, ref in enumerate(piece_refs):
        starts.append(pltpu.make_async_copy(ref, every.at[pl.ds(offset, ref.shape[0])], piece_sems.at[index]))
        offset += ref.shape[0]
    for copy in starts:
        copy.start(priority=1)
    fetched = [pltpu.make_async_copy(ref, to, load_sems.at[index]) for index, (ref, to) in enumerate(zip(load_refs, loads))]
    for copy in fetched:
        copy.start()
    if not turned:
        fetch.wait()
        codes[...] = arrived[:, 0, :].astype(F32).astype(jnp.int32)
        store = pltpu.make_async_copy(codes, got, code_sems.at[1])
        store.start()

    def clear(row, carry):
        acc[row] = jnp.zeros(acc.shape[1:], F32)
        return carry

    if not turned:
        lax.fori_loop(0, acc.shape[0], clear, 0)
        store.wait()
        list_products(info_ref, listing_ref, got, list_ref, blocks)

    def begin_away(index, carry):
        place = jnp.bitwise_and(jnp.right_shift(list_ref[index], 5), 63)
        pltpu.make_async_copy(away_ref.at[place], tiles.at[index], tile_sems.at[index]).start()
        return carry

    def begin_arrived(index, carry):
        device, rank = split(jnp.bitwise_and(jnp.right_shift(list_ref[index], 5), 63), CAP)
        rows = pl.ds(pl.multiple_of(rank * part, part), part)
        parity = jnp.bitwise_and(plane, 1)

        def bring(ref, at, step):
            to = tiles.at[index, pl.ds(pl.multiple_of(step * part, part), part), :]
            pltpu.make_async_copy(ref.at[at, rows, :], to, tile_sems.at[index]).start()

        bring(arrived_ref, device, parity)

        @pl.when(device < devices)
        def first():
            bring(other_a_ref, device, 1 - parity)

        @pl.when(device >= devices)
        def second():
            bring(other_b_ref, device - devices, 1 - parity)

        return carry

    middle, end = list_ref[last], list_ref[last + 1]
    lax.fori_loop(0, middle * BATCH, begin_away, 0)
    lax.fori_loop(middle * BATCH, end * BATCH, begin_arrived, 0)
    if turned:
        lax.fori_loop(0, acc.shape[0], clear, 0)
    for copy in fetched:
        copy.wait()
    for kind in range(3):
        for step in range(planes):
            span = slice(step * side, (step + 1) * side)
            if turned:
                at = pl.ds(pl.multiple_of(jnp.bitwise_and(plane + step, planes - 1) * side, side), side)
                weights[kind, span, :] = loads[3 + kind][at, :]
            else:
                weights[kind, :, span] = loads[3 + step][kind * side : (kind + 1) * side, :]
    for copy in starts:
        copy.wait()

    def add_batch(batch, carry):
        indices = [batch * BATCH + index for index in range(BATCH)]
        codes = [list_ref[index] for index in indices]
        for index in indices:
            pltpu.make_async_copy(away_ref.at[0], tiles.at[index], tile_sems.at[index]).wait()
        products = [
            jnp.dot(tiles[index], every[jnp.right_shift(code, 11)], preferred_element_type=F32) for index, code in zip(indices, codes)
        ]
        for code, product in zip(codes, products):
            row = jnp.bitwise_and(code, 31)
            acc[row] = acc[row] + product
        return carry

    lax.fori_loop(0, end, add_batch, 0)

    def sums(block):
        at = pl.ds(pl.multiple_of(block * side, side), side)
        return (acc[block] + base_out[at, :]).astype(BF16), (acc[blocks + block] + base_in[at, :]).astype(BF16), at

    def times(values, kind):
        return lax.dot_general(values, weights[kind], (((1,), (1 if turned else 0,)), ((), ())), preferred_element_type=F32)

    def multiply(low):
        def at_block(block, carry):
            out, into, at = sums(block)
            to = pl.ds(pl.multiple_of((block - low) * side, side), side)
            if not turned:
                stores[7][at, :] = out
                stores[8][at, :] = into
            part = (times(out, 0) + times(into, 1)) * (1.0 / 32.0) + times(loads[2][at, :], 2)
            stores[0][at, :] = part[:, :side]
            for index in range(3):
                ref = stores[1 + 2 * index + (low > 0)]
                ref[to, :] = part[:, (index + 1) * side : (index + 2) * side].astype(ref.dtype)
            return carry

        return at_block

    written = [pltpu.make_async_copy(ref, to, store_sems.at[index]) for index, (ref, to) in enumerate(zip(stores, store_refs))]
    lax.fori_loop(0, half, multiply(0), 0)
    for index in (3, 1, 5):
        written[index].start()
    lax.fori_loop(half, blocks, multiply(half), 0)
    for index in (4, 2, 6, 0) if turned else (4, 2, 6, 0, 7, 8):
        written[index].start()
    for copy in written:
        copy.wait()


def spread(info, listing, base_out, base_in, others, arrived, others_a_b, away, pieces, turned):
    side, places = away.shape[1], away.shape[0]
    rows, width = base_out.shape
    blocks = rows // side
    planes = 4
    entries = 2 * (places + BATCH)
    every = sum(piece.shape[0] for piece in pieces) // side
    smem = pl.BlockSpec(memory_space=pltpu.SMEM)
    far = pl.BlockSpec(memory_space=pltpu.HBM)
    pieces = [piece.reshape(-1, side, width) for piece in pieces]
    loads = [base_out, base_in, *others]

    def shape(count, kind):
        return jax.ShapeDtypeStruct((count, width), kind)

    devices = places // CAP
    out_shape = [shape(rows, F32)] + [shape(rows // 2, kind) for kind in (F32, BF16, BF16, BF16, BF16, F32)]
    if not turned:
        out_shape += [shape(rows, BF16), shape(rows, BF16)]
    scratch = [pltpu.VMEM(part.shape, part.dtype) for part in loads + out_shape]
    scratch += [
        pltpu.VMEM((2 * blocks + 1, side, width), F32),
        pltpu.VMEM((every, side, width), BF16),
        pltpu.VMEM((entries, side, side), BF16),
        pltpu.VMEM((3, planes * width, width) if turned else (3, width, planes * width), BF16),
        pltpu.SemaphoreType.DMA((len(pieces),)),
        pltpu.SemaphoreType.DMA((entries,)),
        pltpu.SemaphoreType.DMA((len(loads),)),
        pltpu.SemaphoreType.DMA((len(out_shape),)),
    ]
    out_specs = [far] * len(out_shape)
    if not turned:
        out_shape += [jax.ShapeDtypeStruct((entries + 2,), jnp.int32)]
        out_specs += [smem]
        scratch += [
            pltpu.VMEM((devices, CODES, side), BF16),
            pltpu.VMEM((devices, side), jnp.int32),
            pltpu.SMEM((devices, side), jnp.int32),
            pltpu.SemaphoreType.DMA((2,)),
        ]
    return pl.pallas_call(
        lambda *refs: spread_kernel(turned, len(pieces), *refs),
        in_specs=[smem] * 2 + [far] * (len(loads) + 4 + len(pieces)),
        out_specs=out_specs,
        out_shape=out_shape,
        scratch_shapes=scratch,
        compiler_params=pltpu.CompilerParams(vmem_limit_bytes=ROOM),
        cost_estimate=pl.CostEstimate(flops=2 * rows * width * 3 * 512 + places * side**3 * 2, bytes_accessed=16 * MIB, transcendentals=0),
        name="spread",
    )(info, listing, *loads, arrived, *others_a_b, away, *pieces)


def slopes_kernel(left_1_ref, left_2_ref, left_3_ref, z0_ref, z1_ref, z2_ref, z3_ref, out_ref, right):
    width = z0_ref.shape[1]
    planes = right.shape[1] // width
    strips = out_ref.shape[0] // planes
    slivers = out_ref.shape[1] // 3
    for step, ref in enumerate((z0_ref, z1_ref, z2_ref, z3_ref)):
        right[:, step * width : (step + 1) * width] = ref[...]
    for kind, ref in enumerate((left_1_ref, left_2_ref, left_3_ref)):
        terms = lax.dot_general(ref[...], right[...], (((0,), (0,)), ((), ())), preferred_element_type=F32)
        for step in range(planes):
            for strip in range(strips):
                out_ref[step * strips + strip, kind * slivers : (kind + 1) * slivers, :] = terms[
                    strip * slivers : (strip + 1) * slivers, step * width : (step + 1) * width
                ]


def slopes(lefts, rights, devices):
    rows, width = rights[0].shape
    vmem = pl.BlockSpec(memory_space=pltpu.VMEM)
    planes = len(rights)
    return pl.pallas_call(
        slopes_kernel,
        in_specs=[vmem] * 7,
        out_specs=vmem,
        out_shape=jax.ShapeDtypeStruct((devices, 3 * width * planes // devices, width), F32),
        scratch_shapes=[pltpu.VMEM((rows, planes * width), BF16)],
        compiler_params=pltpu.CompilerParams(vmem_limit_bytes=LESS),
        cost_estimate=pl.CostEstimate(flops=2 * rows * 3 * width * planes * width, bytes_accessed=3 * MIB, transcendentals=0),
        name="slopes",
    )(*lefts, *rights)


def around(devices, stage, step):
    pairs = []
    for here in range(devices):
        core, x, y = here % 2, here // 2 % 4, here // 8
        if (core + stage) % 2 == 0:
            x = (x + step) % 4
        else:
            y = (y + step) % 4
        pairs.append((here, (y * 4 + x) * 2 + core))
    return pairs


def sister(part, devices):
    return lax.ppermute(part, "nodes", [(here, here ^ 1) for here in range(devices)])


def gather(values, devices, before, between):
    def move(part, stage, step):
        return lax.ppermute(part, "nodes", around(devices, stage, step))

    plus, minus, far = move(values, 0, 1), move(values, 0, -1), move(values, 0, 2)
    row = jnp.concatenate([values, plus, far, minus])
    row, before = lax.optimization_barrier((row, before))
    plus, minus = move(row, 1, 1), move(row, 1, -1)
    plus, minus, between = lax.optimization_barrier((plus, minus, between(before)))
    half = row.shape[0] // 2
    plus_far, minus_far = move(plus[:half], 1, 1), move(minus[half:], 1, -1)
    own = [row, plus, plus_far, minus_far, minus]
    return own + [sister(piece, devices) for piece in own], before, between


def shards(
    node_features, w_out, w_in, w_self, cotangent, tile_src, tile_dst, tile_pattern, tile_count
):
    devices = lax.axis_size("nodes")
    planes = lax.axis_size("hid")
    myself = lax.axis_index("nodes").astype(jnp.int32)
    plane = lax.axis_index("hid").astype(jnp.int32)
    core = lax.rem(myself, 2)
    side = tile_pattern.shape[1]
    rows, width = node_features.shape
    blocks = rows // side
    halves = rows // 2

    def shift(values, step):
        return lax.ppermute(values, "hid", [(here, (here + step) % planes) for here in range(planes)])

    info = jnp.stack([tile_count[0], myself, plane, lax.rem(lax.div(myself, 2), 4), lax.div(myself, 8), core])
    away, send, sent = pick(tile_src, tile_dst, info, tile_pattern, blocks, devices)
    stacked = jnp.stack([w_out, w_in, w_self]).reshape(3, planes, width, width)

    def rows_of(step):
        return lax.dynamic_index_in_dim(stacked, (plane + step) % planes, 1, keepdims=False).reshape(3 * width, width)

    pieces_x, _, (local, base_out, base_in) = gather(
        node_features,
        devices,
        (info, node_features, send),
        lambda held: pile(tile_src, tile_dst, held[0], tile_pattern, held[1]),
    )
    forward = [rows_of(0)] + [shift(rows_of(-step), -step) for step in range(1, planes)]
    arrived = lax.all_to_all(send, "nodes", 0, 0, tiled=True)
    arrived, _ = lax.optimization_barrier((arrived, base_out))
    middle = devices // 2
    others = [
        lax.ppermute(arrived[:middle], "hid", [(here, here ^ 1) for here in range(planes)]),
        lax.ppermute(arrived[middle:], "hid", [(here, (here + 1 if here % 2 else here - 1) % planes) for here in range(planes)]),
    ]
    base_out, forward = lax.optimization_barrier((base_out, forward))

    def collect(own, p1a, p1b, p2a, p2b, p3a, p3b, give=False):
        left, right = shift(p2a, 1), shift(p2b, -1)
        one_b, three_a = shift(p1b, 1), shift(p3a, -1)
        one_a = shift((p1a + left.astype(F32)).astype(BF16), 1)
        three_b = shift((p3b + right.astype(F32)).astype(BF16), -1)
        low = own[:halves] + one_a.astype(F32) + three_a.astype(F32)
        high = own[halves:] + one_b.astype(F32) + three_b.astype(F32)
        return (jnp.concatenate([low, high]), (one_b, three_a)) if give else jnp.concatenate([low, high])

    *parts, prop_out, prop_in, listed = spread(
        info, sent, base_out, base_in, [node_features, *forward], arrived, others, away, pieces_x, False
    )
    pre_act = collect(*parts)
    hidden = jax.nn.silu(pre_act).astype(BF16)
    gate = jax.nn.sigmoid(pre_act)
    grad_z = (cotangent.astype(F32) * gate * (1.0 + pre_act * (1.0 - gate))).astype(BF16)

    rights = [grad_z] + [shift(grad_z, step) for step in range(1, planes)]
    base_out = jnp.dot(local, grad_z, preferred_element_type=F32)
    base_in = jnp.einsum("ij,ik->jk", local, grad_z, preferred_element_type=F32)
    slivers = width * planes // devices
    pieces_z, (base_out, base_in), _ = gather(grad_z, devices, (base_out, base_in), lambda held: ())
    terms = slopes([prop_out, prop_in, node_features], rights, devices)
    terms = lax.all_to_all(terms, "nodes", 0, 0, tiled=True)
    parts = spread(info, listed, base_out, base_in, [grad_z, w_in, w_out, w_self], arrived, others, away, pieces_z, True)
    grad_sum, middle_sum = collect(*parts, True)
    grad_input = grad_sum.astype(BF16)

    strips = width // slivers
    moves = [
        ((step * strips + strip) * planes + here, (here * strips + strip) * planes + (here - step) % planes)
        for step in range(planes)
        for strip in range(strips)
        for here in range(planes)
    ]
    summed, _ = lax.optimization_barrier((jnp.sum(terms, axis=0), middle_sum))
    grads = lax.ppermute(summed, ("nodes", "hid"), moves).reshape(3, slivers, width)
    return (hidden, grad_input, grads[0] / 32.0, grads[1] / 32.0, grads[2])


def solution(mesh):
    in_specs = (
        P("nodes", "hid"),
        P(None, "hid"),
        P(None, "hid"),
        P(None, "hid"),
        P("nodes", "hid"),
        P("nodes"),
        P("nodes"),
        P("nodes", None, None),
        P("nodes"),
    )
    out_specs = (
        P("nodes", "hid"),
        P("nodes", "hid"),
        P("nodes", "hid"),
        P("nodes", "hid"),
        P("nodes", "hid"),
    )
    return jax.shard_map(shards, mesh=mesh, in_specs=in_specs, out_specs=out_specs, check_vma=False)
```

```python
import jax
import jax.numpy as jnp
from jax import lax
from jax.experimental import pallas as pl
from jax.experimental.pallas import tpu as pltpu
from jax.sharding import PartitionSpec as P

CAP = 2
GROUP = 16
BATCH = 8
CODES = 16
PICKS = 8
MIB = 1024 * 1024
ROOM = 63 * MIB
LESS = 16 * MIB
F32 = jnp.float32
BF16 = jnp.bfloat16


def split(value, size):
    shift = size.bit_length() - 1
    return jnp.right_shift(value, shift), jnp.bitwise_and(value, size - 1)


def pick_kernel(blocks, src_ref, dst_ref, info_ref, pattern_ref, away_ref, send_ref, meta_ref, tiles, counts, listed, sems):
    side = tiles.shape[1]
    devices = counts.shape[0]
    part = (send_ref.shape[1] - CODES) // CAP
    total, myself, first_row = info_ref[0], info_ref[1], jnp.bitwise_and(info_ref[2], 1) * part

    def clear(owner, carry):
        counts[owner] = 0
        for rank in range(CAP):
            meta_ref[owner * CAP + rank] = 0
        return carry

    lax.fori_loop(0, devices, clear, 0, unroll=4)

    def copy(slot, entry):
        return pltpu.make_async_copy(pattern_ref.at[slot], tiles.at[entry], sems.at[entry])

    def scan(slot, found):
        owner, _ = split(dst_ref[slot], blocks)
        listed[found] = slot
        return found + ((owner != myself) & (slot < total)).astype(jnp.int32)

    found = lax.fori_loop(0, dst_ref.shape[0], scan, 0, unroll=32)
    found = jnp.minimum(found, devices * CAP)

    def keep(entry, carry):
        slot = listed[entry]
        copy(slot, entry).start()
        owner, landing = split(dst_ref[slot], blocks)
        source = jnp.clip(src_ref[slot] - myself * blocks, 0, blocks - 1)
        rank = jnp.minimum(counts[owner], CAP - 1)
        counts[owner] = rank + 1
        place = owner * CAP + rank
        meta_ref[place] = 1 + source + blocks * landing
        listed[entry] = place
        return carry

    lax.fori_loop(0, found, keep, 0)
    row = lax.broadcasted_iota(jnp.int32, (part, side), 0)
    column = lax.broadcasted_iota(jnp.int32, (part, side), 1)
    chosen = (column == row + first_row).astype(F32).astype(BF16)

    def turn(batch, carry):
        first = batch * PICKS
        for index in range(PICKS):

            @pl.when(first + index < found)
            def arrive():
                copy(0, first + index).wait()

        entries = [jnp.minimum(first + index, found - 1) for index in range(PICKS)]
        values = [tiles[entry].astype(F32).astype(BF16) for entry in entries]
        turned = [
            lax.dot_general(chosen, value, (((1,), (1,)), ((), ())), preferred_element_type=F32).astype(BF16) for value in values
        ]
        for index, entry in enumerate(entries):
            place = listed[entry]
            owner, rank = split(place, CAP)
            away_ref[place] = values[index]
            send_ref[owner, pl.ds(pl.multiple_of(rank * part, part), part), :] = turned[index]
        return carry

    lax.fori_loop(0, lax.div(found + PICKS - 1, PICKS), turn, 0)
    lane = lax.broadcasted_iota(jnp.int32, (CODES, side), 1)

    def code(owner, carry):
        values = jnp.zeros((CODES, side), jnp.int32)
        for rank in range(CAP):
            values = jnp.where(lane == rank, meta_ref[owner * CAP + rank], values)
        send_ref[owner, CAP * part :, :] = values.astype(F32).astype(BF16)
        return carry

    lax.fori_loop(0, devices, code, 0, unroll=4)


def pick(tile_src, tile_dst, info, tile_pattern, blocks, devices):
    side = tile_pattern.shape[1]
    places = devices * CAP
    vmem = pl.BlockSpec(memory_space=pltpu.VMEM)
    smem = pl.BlockSpec(memory_space=pltpu.SMEM)
    return pl.pallas_call(
        lambda *refs: pick_kernel(blocks, *refs),
        in_specs=[smem, smem, smem, pl.BlockSpec(memory_space=pltpu.HBM)],
        out_specs=[vmem, vmem, smem],
        out_shape=[
            jax.ShapeDtypeStruct((places, side, side), BF16),
            jax.ShapeDtypeStruct((devices, CAP * side // 2 + CODES, side), BF16),
            jax.ShapeDtypeStruct((places,), jnp.int32),
        ],
        scratch_shapes=[
            pltpu.VMEM((places, side, side), jnp.int32),
            pltpu.SMEM((devices,), jnp.int32),
            pltpu.SMEM((tile_src.shape[0] + 1,), jnp.int32),
            pltpu.SemaphoreType.DMA((places,)),
        ],
        compiler_params=pltpu.CompilerParams(vmem_limit_bytes=ROOM),
        cost_estimate=pl.CostEstimate(flops=places * side * side, bytes_accessed=8 * MIB, transcendentals=0),
        name="pick",
    )(tile_src, tile_dst, info, tile_pattern)


def own_products(local_ref, values_ref, out_ref, in_ref):
    side = values_ref.shape[1]

    def block(index, carry):
        at = pl.ds(pl.multiple_of(index * side, side), side)
        out_ref[at, :] = jnp.dot(local_ref[at, :], values_ref[...], preferred_element_type=F32)
        return carry

    lax.fori_loop(0, values_ref.shape[0] // side, block, 0)
    for index in range(values_ref.shape[0] // side):
        span = slice(index * side, (index + 1) * side)
        in_ref[span, :] = lax.dot_general(local_ref[:, span], values_ref[...], (((0,), (0,)), ((), ())), preferred_element_type=F32)


def pile_kernel(src_ref, dst_ref, info_ref, pattern_ref, values_ref, local_ref, out_ref, in_ref, acc, groups, sems):
    depth, group, side = groups.shape[0], groups.shape[1], groups.shape[2]
    blocks = local_ref.shape[0] // side
    total, myself = info_ref[0], info_ref[1]
    turns = lax.div(total + group - 1, group)

    def copy(turn):
        return pltpu.make_async_copy(pattern_ref.at[pl.ds(turn * group, group)], groups.at[turn], sems.at[turn])

    for turn in range(depth):

        @pl.when(turn < turns)
        def begin():
            copy(turn).start()

    def clear(pair, carry):
        acc[pair] = jnp.zeros((side, side), jnp.int32)
        return carry

    lax.fori_loop(0, acc.shape[0], clear, 0)

    def take(turn, carry):
        copy(turn).wait()

        def add(index, carry):
            slot = turn * group + index
            source = jnp.clip(src_ref[slot] - myself * blocks, 0, blocks - 1)
            owner, landing = split(dst_ref[slot], blocks)
            pair = jnp.where((owner == myself) & (slot < total), source * blocks + landing, blocks * blocks)
            acc[pair] = acc[pair] + groups[turn, index]
            return carry

        lax.fori_loop(0, group, add, 0, unroll=4)
        return carry

    lax.fori_loop(0, turns, take, 0)

    def finish(source, carry):
        rows = pl.ds(pl.multiple_of(source * side, side), side)
        for landing in range(blocks):
            local_ref[rows, landing * side : (landing + 1) * side] = acc[source * blocks + landing].astype(F32).astype(BF16)
        return carry

    lax.fori_loop(0, blocks, finish, 0)
    own_products(local_ref, values_ref, out_ref, in_ref)


def pile(tile_src, tile_dst, info, tile_pattern, values):
    slots, side = tile_pattern.shape[0], tile_pattern.shape[1]
    blocks = values.shape[0] // side
    smem = pl.BlockSpec(memory_space=pltpu.SMEM)
    vmem = pl.BlockSpec(memory_space=pltpu.VMEM)
    return pl.pallas_call(
        pile_kernel,
        in_specs=[smem, smem, smem, pl.BlockSpec(memory_space=pltpu.HBM), vmem],
        out_specs=[vmem] * 3,
        out_shape=[jax.ShapeDtypeStruct((blocks * side, blocks * side), BF16)] + [jax.ShapeDtypeStruct(values.shape, F32)] * 2,
        scratch_shapes=[
            pltpu.VMEM((blocks * blocks + 1, side, side), jnp.int32),
            pltpu.VMEM((slots // GROUP, GROUP, side, side), jnp.int32),
            pltpu.SemaphoreType.DMA((slots // GROUP,)),
        ],
        compiler_params=pltpu.CompilerParams(vmem_limit_bytes=ROOM),
        cost_estimate=pl.CostEstimate(flops=slots * side * side, bytes_accessed=slots * side * side * 4, transcendentals=0),
        name="pile",
    )(tile_src, tile_dst, info, tile_pattern, values)


def list_products(info_ref, sent_ref, got_ref, list_ref, blocks):
    x, y, core = info_ref[3], info_ref[4], info_ref[5]
    places = sent_ref.shape[0]
    last = list_ref.shape[0] - 2

    def entry(device, block, place, row):
        chip, their_core = split(device, 2)
        their_y, their_x = split(chip, 4)
        step_x, step_y = jnp.bitwise_and(x - their_x, 3), jnp.bitwise_and(y - their_y, 3)
        first = jnp.where(their_core == 0, step_x, step_y)
        second = jnp.where(their_core == 0, step_y, step_x)
        index = (second * 4 + first) * blocks + block + jnp.where(their_core == core, 0, 16 * blocks)
        return (index * 64 + place) * 32 + row

    def out(place, count):
        code = sent_ref[place] - 1
        landing, source = split(jnp.maximum(code, 0), blocks)
        list_ref[count] = entry(jnp.right_shift(place, 1), landing, place, source)
        return count + (code >= 0).astype(jnp.int32)

    def into(place, count):
        code = got_ref[jnp.right_shift(place, 1), jnp.bitwise_and(place, 1)] - 1
        landing, source = split(jnp.maximum(code, 0), blocks)
        list_ref[count] = entry(jnp.right_shift(place, 1), source, place, blocks + landing)
        return count + (code >= 0).astype(jnp.int32)

    def padded(count):
        ends = lax.div(count + BATCH - 1, BATCH) * BATCH

        def pad(index, carry):
            list_ref[index] = 2 * blocks
            return carry

        lax.fori_loop(count, ends, pad, 0)
        return ends

    count = padded(lax.fori_loop(0, places, out, 0, unroll=4))
    list_ref[last] = lax.div(count, BATCH)
    count = padded(lax.fori_loop(0, places, into, count, unroll=4))
    list_ref[last + 1] = lax.div(count, BATCH)


def spread_kernel(turned, n_pieces, *refs):
    info_ref, listing_ref, refs = refs[0], refs[1], refs[2:]
    n_loads, n_stores = (6, 7) if turned else (7, 9)
    load_refs, refs = refs[:n_loads], refs[n_loads:]
    (arrived_ref, other_a_ref, other_b_ref, away_ref), refs = refs[:4], refs[4:]
    piece_refs, store_refs, refs = refs[:n_pieces], refs[n_pieces : n_pieces + n_stores], refs[n_pieces + n_stores :]
    if turned:
        list_ref = listing_ref
    else:
        list_ref, refs = refs[0], refs[1:]
    loads, refs = refs[:n_loads], refs[n_loads:]
    stores, refs = refs[:n_stores], refs[n_stores:]
    acc, every, tiles, weights, piece_sems, tile_sems, load_sems, store_sems = refs[:8]
    refs = refs[8:]
    base_out, base_in = loads[:2]
    side = every.shape[1]
    blocks = base_out.shape[0] // side
    plane = info_ref[2]
    planes = 4
    half, part, devices = blocks // 2, side // 2, other_a_ref.shape[0]
    last = list_ref.shape[0] - 2
    if not turned:
        arrived, codes, got, code_sems = refs
        fetch = pltpu.make_async_copy(arrived_ref.at[:, pl.ds(CAP * part, CODES), :], arrived, code_sems.at[0])
        fetch.start()
    starts = []
    offset = 0
    for index, ref in enumerate(piece_refs):
        starts.append(pltpu.make_async_copy(ref, every.at[pl.ds(offset, ref.shape[0])], piece_sems.at[index]))
        offset += ref.shape[0]
    for copy in starts:
        copy.start(priority=1)
    fetched = [pltpu.make_async_copy(ref, to, load_sems.at[index]) for index, (ref, to) in enumerate(zip(load_refs, loads))]
    for copy in fetched:
        copy.start()
    if not turned:
        fetch.wait()
        codes[...] = arrived[:, 0, :].astype(F32).astype(jnp.int32)
        store = pltpu.make_async_copy(codes, got, code_sems.at[1])
        store.start()

    def clear(row, carry):
        acc[row] = jnp.zeros(acc.shape[1:], F32)
        return carry

    if not turned:
        lax.fori_loop(0, acc.shape[0], clear, 0)
        store.wait()
        list_products(info_ref, listing_ref, got, list_ref, blocks)

    def begin_away(index, carry):
        place = jnp.bitwise_and(jnp.right_shift(list_ref[index], 5), 63)
        pltpu.make_async_copy(away_ref.at[place], tiles.at[index], tile_sems.at[index]).start()
        return carry

    def begin_arrived(index, carry):
        device, rank = split(jnp.bitwise_and(jnp.right_shift(list_ref[index], 5), 63), CAP)
        rows = pl.ds(pl.multiple_of(rank * part, part), part)
        parity = jnp.bitwise_and(plane, 1)

        def bring(ref, at, step):
            to = tiles.at[index, pl.ds(pl.multiple_of(step * part, part), part), :]
            pltpu.make_async_copy(ref.at[at, rows, :], to, tile_sems.at[index]).start()

        bring(arrived_ref, device, parity)

        @pl.when(device < devices)
        def first():
            bring(other_a_ref, device, 1 - parity)

        @pl.when(device >= devices)
        def second():
            bring(other_b_ref, device - devices, 1 - parity)

        return carry

    middle, end = list_ref[last], list_ref[last + 1]
    lax.fori_loop(0, middle * BATCH, begin_away, 0)
    lax.fori_loop(middle * BATCH, end * BATCH, begin_arrived, 0)
    if turned:
        lax.fori_loop(0, acc.shape[0], clear, 0)
    for copy in fetched:
        copy.wait()
    for kind in range(3):
        for step in range(planes):
            span = slice(step * side, (step + 1) * side)
            if turned:
                at = pl.ds(pl.multiple_of(jnp.bitwise_and(plane + step, planes - 1) * side, side), side)
                weights[kind, span, :] = loads[3 + kind][at, :]
            else:
                weights[kind, :, span] = loads[3 + step][kind * side : (kind + 1) * side, :]
    for copy in starts:
        copy.wait()

    def add_batch(batch, carry):
        indices = [batch * BATCH + index for index in range(BATCH)]
        codes = [list_ref[index] for index in indices]
        for index in indices:
            pltpu.make_async_copy(away_ref.at[0], tiles.at[index], tile_sems.at[index]).wait()
        products = [
            jnp.dot(tiles[index], every[jnp.right_shift(code, 11)], preferred_element_type=F32) for index, code in zip(indices, codes)
        ]
        for code, product in zip(codes, products):
            row = jnp.bitwise_and(code, 31)
            acc[row] = acc[row] + product
        return carry

    lax.fori_loop(0, end, add_batch, 0)

    def sums(block):
        at = pl.ds(pl.multiple_of(block * side, side), side)
        return (acc[block] + base_out[at, :]).astype(BF16), (acc[blocks + block] + base_in[at, :]).astype(BF16), at

    def times(values, kind):
        return lax.dot_general(values, weights[kind], (((1,), (1 if turned else 0,)), ((), ())), preferred_element_type=F32)

    def multiply(low):
        def at_block(block, carry):
            out, into, at = sums(block)
            to = pl.ds(pl.multiple_of((block - low) * side, side), side)
            if not turned:
                stores[7][at, :] = out
                stores[8][at, :] = into
            part = (times(out, 0) + times(into, 1)) * (1.0 / 32.0) + times(loads[2][at, :], 2)
            stores[0][at, :] = part[:, :side]
            for index in range(3):
                ref = stores[1 + 2 * index + (low > 0)]
                ref[to, :] = part[:, (index + 1) * side : (index + 2) * side].astype(ref.dtype)
            return carry

        return at_block

    written = [pltpu.make_async_copy(ref, to, store_sems.at[index]) for index, (ref, to) in enumerate(zip(stores, store_refs))]
    lax.fori_loop(0, half, multiply(0), 0)
    for index in (3, 1, 5):
        written[index].start()
    lax.fori_loop(half, blocks, multiply(half), 0)
    for index in (4, 2, 6, 0) if turned else (4, 2, 6, 0, 7, 8):
        written[index].start()
    for copy in written:
        copy.wait()


def spread(info, listing, base_out, base_in, others, arrived, others_a_b, away, pieces, turned):
    side, places = away.shape[1], away.shape[0]
    rows, width = base_out.shape
    blocks = rows // side
    planes = 4
    entries = 2 * (places + BATCH)
    every = sum(piece.shape[0] for piece in pieces) // side
    smem = pl.BlockSpec(memory_space=pltpu.SMEM)
    far = pl.BlockSpec(memory_space=pltpu.HBM)
    pieces = [piece.reshape(-1, side, width) for piece in pieces]
    loads = [base_out, base_in, *others]

    def shape(count, kind):
        return jax.ShapeDtypeStruct((count, width), kind)

    devices = places // CAP
    out_shape = [shape(rows, F32)] + [shape(rows // 2, kind) for kind in (F32, BF16, BF16, BF16, BF16, F32)]
    if not turned:
        out_shape += [shape(rows, BF16), shape(rows, BF16)]
    scratch = [pltpu.VMEM(part.shape, part.dtype) for part in loads + out_shape]
    scratch += [
        pltpu.VMEM((2 * blocks + 1, side, width), F32),
        pltpu.VMEM((every, side, width), BF16),
        pltpu.VMEM((entries, side, side), BF16),
        pltpu.VMEM((3, planes * width, width) if turned else (3, width, planes * width), BF16),
        pltpu.SemaphoreType.DMA((len(pieces),)),
        pltpu.SemaphoreType.DMA((entries,)),
        pltpu.SemaphoreType.DMA((len(loads),)),
        pltpu.SemaphoreType.DMA((len(out_shape),)),
    ]
    out_specs = [far] * len(out_shape)
    if not turned:
        out_shape += [jax.ShapeDtypeStruct((entries + 2,), jnp.int32)]
        out_specs += [smem]
        scratch += [
            pltpu.VMEM((devices, CODES, side), BF16),
            pltpu.VMEM((devices, side), jnp.int32),
            pltpu.SMEM((devices, side), jnp.int32),
            pltpu.SemaphoreType.DMA((2,)),
        ]
    return pl.pallas_call(
        lambda *refs: spread_kernel(turned, len(pieces), *refs),
        in_specs=[smem] * 2 + [far] * (len(loads) + 4 + len(pieces)),
        out_specs=out_specs,
        out_shape=out_shape,
        scratch_shapes=scratch,
        compiler_params=pltpu.CompilerParams(vmem_limit_bytes=ROOM),
        cost_estimate=pl.CostEstimate(flops=2 * rows * width * 3 * 512 + places * side**3 * 2, bytes_accessed=16 * MIB, transcendentals=0),
        name="spread",
    )(info, listing, *loads, arrived, *others_a_b, away, *pieces)


def slopes_kernel(left_1_ref, left_2_ref, left_3_ref, z0_ref, z1_ref, z2_ref, z3_ref, out_ref, right):
    width = z0_ref.shape[1]
    planes = right.shape[1] // width
    strips = out_ref.shape[0] // planes
    slivers = out_ref.shape[1] // 3
    for step, ref in enumerate((z0_ref, z1_ref, z2_ref, z3_ref)):
        right[:, step * width : (step + 1) * width] = ref[...]
    for kind, ref in enumerate((left_1_ref, left_2_ref, left_3_ref)):
        terms = lax.dot_general(ref[...], right[...], (((0,), (0,)), ((), ())), preferred_element_type=F32)
        for step in range(planes):
            for strip in range(strips):
                out_ref[step * strips + strip, kind * slivers : (kind + 1) * slivers, :] = terms[
                    strip * slivers : (strip + 1) * slivers, step * width : (step + 1) * width
                ]


def slopes(lefts, rights, devices):
    rows, width = rights[0].shape
    vmem = pl.BlockSpec(memory_space=pltpu.VMEM)
    planes = len(rights)
    return pl.pallas_call(
        slopes_kernel,
        in_specs=[vmem] * 7,
        out_specs=vmem,
        out_shape=jax.ShapeDtypeStruct((devices, 3 * width * planes // devices, width), F32),
        scratch_shapes=[pltpu.VMEM((rows, planes * width), BF16)],
        compiler_params=pltpu.CompilerParams(vmem_limit_bytes=LESS),
        cost_estimate=pl.CostEstimate(flops=2 * rows * 3 * width * planes * width, bytes_accessed=3 * MIB, transcendentals=0),
        name="slopes",
    )(*lefts, *rights)


def around(devices, stage, step):
    pairs = []
    for here in range(devices):
        core, x, y = here % 2, here // 2 % 4, here // 8
        if (core + stage) % 2 == 0:
            x = (x + step) % 4
        else:
            y = (y + step) % 4
        pairs.append((here, (y * 4 + x) * 2 + core))
    return pairs


def sister(part, devices):
    return lax.ppermute(part, "nodes", [(here, here ^ 1) for here in range(devices)])


def gather(values, devices, before, between):
    def move(part, stage, step):
        return lax.ppermute(part, "nodes", around(devices, stage, step))

    plus, minus, far = move(values, 0, 1), move(values, 0, -1), move(values, 0, 2)
    row = jnp.concatenate([values, plus, far, minus])
    row, before = lax.optimization_barrier((row, before))
    plus, minus = move(row, 1, 1), move(row, 1, -1)
    plus, minus, between = lax.optimization_barrier((plus, minus, between(before)))
    half = row.shape[0] // 2
    plus_far, minus_far = move(plus[:half], 1, 1), move(minus[half:], 1, -1)
    own = [row, plus, plus_far, minus_far, minus]
    return own + [sister(piece, devices) for piece in own], before, between


def shards(
    node_features, w_out, w_in, w_self, cotangent, tile_src, tile_dst, tile_pattern, tile_count
):
    devices = lax.axis_size("nodes")
    planes = lax.axis_size("hid")
    myself = lax.axis_index("nodes").astype(jnp.int32)
    plane = lax.axis_index("hid").astype(jnp.int32)
    core = lax.rem(myself, 2)
    side = tile_pattern.shape[1]
    rows, width = node_features.shape
    blocks = rows // side
    halves = rows // 2

    def shift(values, step):
        return lax.ppermute(values, "hid", [(here, (here + step) % planes) for here in range(planes)])

    info = jnp.stack([tile_count[0], myself, plane, lax.rem(lax.div(myself, 2), 4), lax.div(myself, 8), core])
    away, send, sent = pick(tile_src, tile_dst, info, tile_pattern, blocks, devices)
    stacked = jnp.stack([w_out, w_in, w_self]).reshape(3, planes, width, width)

    def rows_of(step):
        return lax.dynamic_index_in_dim(stacked, (plane + step) % planes, 1, keepdims=False).reshape(3 * width, width)

    pieces_x, _, (local, base_out, base_in) = gather(
        node_features,
        devices,
        (info, node_features, send),
        lambda held: pile(tile_src, tile_dst, held[0], tile_pattern, held[1]),
    )
    forward = [rows_of(0)] + [shift(rows_of(-step), -step) for step in range(1, planes)]
    arrived = lax.all_to_all(send, "nodes", 0, 0, tiled=True)
    arrived, _ = lax.optimization_barrier((arrived, base_out))
    middle = devices // 2
    others = [
        lax.ppermute(arrived[:middle], "hid", [(here, here ^ 1) for here in range(planes)]),
        lax.ppermute(arrived[middle:], "hid", [(here, (here + 1 if here % 2 else here - 1) % planes) for here in range(planes)]),
    ]
    base_out, forward = lax.optimization_barrier((base_out, forward))

    def collect(own, p1a, p1b, p2a, p2b, p3a, p3b, give=False):
        left, right = shift(p2a, 1), shift(p2b, -1)
        one_b, three_a = shift(p1b, 1), shift(p3a, -1)
        one_a = shift((p1a + left.astype(F32)).astype(BF16), 1)
        three_b = shift((p3b + right.astype(F32)).astype(BF16), -1)
        low = own[:halves] + one_a.astype(F32) + three_a.astype(F32)
        high = own[halves:] + one_b.astype(F32) + three_b.astype(F32)
        return (jnp.concatenate([low, high]), (one_b, three_a)) if give else jnp.concatenate([low, high])

    *parts, prop_out, prop_in, listed = spread(
        info, sent, base_out, base_in, [node_features, *forward], arrived, others, away, pieces_x, False
    )
    pre_act = collect(*parts)
    hidden = jax.nn.silu(pre_act).astype(BF16)
    gate = jax.nn.sigmoid(pre_act)
    grad_z = (cotangent.astype(F32) * gate * (1.0 + pre_act * (1.0 - gate))).astype(BF16)

    rights = [grad_z] + [shift(grad_z, step) for step in range(1, planes)]
    base_out = jnp.dot(local, grad_z, preferred_element_type=F32)
    base_in = jnp.einsum("ij,ik->jk", local, grad_z, preferred_element_type=F32)
    slivers = width * planes // devices
    pieces_z, (base_out, base_in), _ = gather(grad_z, devices, (base_out, base_in), lambda held: ())
    terms = slopes([prop_out, prop_in, node_features], rights, devices)
    terms = lax.all_to_all(terms, "nodes", 0, 0, tiled=True)
    parts = spread(info, listed, base_out, base_in, [grad_z, w_in, w_out, w_self], arrived, others, away, pieces_z, True)
    grad_sum, middle_sum = collect(*parts, True)
    grad_input = grad_sum.astype(BF16)

    strips = width // slivers
    moves = [
        ((step * strips + strip) * planes + here, (here * strips + strip) * planes + (here - step) % planes)
        for step in range(planes)
        for strip in range(strips)
        for here in range(planes)
    ]
    summed, _ = lax.optimization_barrier((jnp.sum(terms, axis=0), middle_sum))
    grads = lax.ppermute(summed, ("nodes", "hid"), moves).reshape(3, slivers, width)
    return (hidden, grad_input, grads[0] / 32.0, grads[1] / 32.0, grads[2])


def solution(mesh):
    in_specs = (
        P("nodes", "hid"),
        P(None, "hid"),
        P(None, "hid"),
        P(None, "hid"),
        P("nodes", "hid"),
        P("nodes"),
        P("nodes"),
        P("nodes", None, None),
        P("nodes"),
    )
    out_specs = (
        P("nodes", "hid"),
        P("nodes", "hid"),
        P("nodes", "hid"),
        P("nodes", "hid"),
        P("nodes", "hid"),
    )
    return jax.shard_map(shards, mesh=mesh, in_specs=in_specs, out_specs=out_specs, check_vma=False)
```
